256 devices in a mesh: tile: 64 (over y, z, core), depth: 4 (over x).
Axes of the slice: x: 4, y: 4, z: 8, core: 2. Of those that a mesh axis runs over, the one named last changes fastest.
Arguments:
- object_real: float32 [12, 8192, 256], P('depth', 'tile'), may hold values from 0.75 to 1.05
- object_imag: float32 [12, 8192, 256], P('depth', 'tile'), may hold values from -0.3 to 0.3
- probe_real: float32 [2, 128, 128], replicated, may hold values from -3 to 3
- probe_imag: float32 [2, 128, 128], replicated, may hold values from -3 to 3
- measured: float32 [256, 128, 128], P('tile'), may hold values from 0 to 1.2
- row_offset: int32 [256], P('tile'), may hold values from 0 to 127
- col_offset: int32 [256], P('tile'), may hold values from 0 to 128
- counts: int32 [64], replicated, may hold values from 1 to 4, as said below
Outputs:
- new_object_real: float32 [12, 8192, 256], P('depth', 'tile')
- new_object_imag: float32 [12, 8192, 256], P('depth', 'tile')
- new_probe_real: float32 [2, 128, 128], P(None, 'depth')
- new_probe_imag: float32 [2, 128, 128], P(None, 'depth')
The draws below stay inside these ranges and needn't reach their ends.
Inputs may be any that keep to these rules, and one draw needn't show every extreme that they name: `counts`: live positions of each tile; 4 on at least one tile.
All inputs are finite; a program needn't handle non-finite values.
Results may differ from the reference program's by a relative error of at most 0.0003.
Values sent between devices are 32-bit elements; how exact they have to be, the bound alone decides.
A program may use at most 128 MiB of HBM per device.

```python
import jax
import jax.numpy as jnp
from jax import lax

PIX = 128
MODES = 2
CAP = 4
ROWS_DEV = 128
COLS = 256
SLICES = 12
NROWS = 8192
SLOTS = 256
N_TILE = 64


def draw_counts(key, part):
    key = jax.random.fold_in(key, 11)
    key_one, key_two = jax.random.split(key)
    halvings = jax.random.randint(key_one, (N_TILE,), 0, 4)
    values = jnp.maximum(CAP // 2 ** halvings, 1)
    chosen = jax.random.randint(key_two, (), 0, N_TILE)
    return jnp.where(jnp.arange(N_TILE) == chosen, CAP, values).astype(jnp.int32)


def place_ends(array, own_key, least, largest):
    place = [jax.random.randint(jax.random.fold_in(own_key, axis), (), 0, length) for axis, length in enumerate(array.shape)]
    widest = array.shape.index(max(array.shape))
    beside = place[:widest] + [(place[widest] + 1) % array.shape[widest]] + place[widest + 1:]
    return array.at[tuple(place)].set(least).at[tuple(beside)].set(largest)


def block_scale(stream_key, shape, shards, least, top_value):
    level, own = 1.0, jax.random.fold_in(stream_key, 6)
    for axis_at, blocks in shards:
        draws = jnp.exp(jax.random.uniform(jax.random.fold_in(own, axis_at), (blocks,), jnp.float32, least / len(shards), top_value / len(shards)))
        level = level * jnp.repeat(draws, shape[axis_at] // blocks).reshape([-1 if axis == axis_at else 1 for axis in range(len(shape))])
    return level


def normal_values(rng, dims, scale, limit, held_as=jnp.bfloat16):
    values = jax.random.normal(rng, dims, jnp.float32) * scale
    return jnp.minimum(jnp.maximum(values, -limit), limit).astype(held_as)


def setup_inputs(seed: int = 0) -> dict:
    key_list = jax.random.split(jax.random.key(seed), 9)
    object_real = jnp.clip(0.75 + 0.29999995 * jax.random.uniform(key_list[0], (SLICES, NROWS, COLS), jnp.float32) ** block_scale(key_list[0], (SLICES, NROWS, COLS), ((0, 4), (1, 64)), -0.2, 0.2), 0.75, 1.05)
    object_imag = jnp.clip(jax.random.uniform(key_list[1], (SLICES, NROWS, COLS), jnp.float32, -0.3, 0.3) * block_scale(key_list[1], (SLICES, NROWS, COLS), ((0, 4), (1, 64)), -0.4, 0.0), -0.3, 0.3)
    probe_real = normal_values(key_list[2], (MODES, PIX, PIX), 0.5, 3.0, jnp.float32)
    probe_imag = normal_values(key_list[3], (MODES, PIX, PIX), 0.5, 3.0, jnp.float32)
    measured = jnp.clip(1.2 * jax.random.uniform(key_list[4], (SLOTS, PIX, PIX), jnp.float32) ** block_scale(key_list[4], (SLOTS, PIX, PIX), ((0, 64),), -0.2, 0.2), 0.0, 1.2)
    row_offset = place_ends(jax.random.randint(key_list[5], (SLOTS,), 0, ROWS_DEV), jax.random.fold_in(key_list[5], 1), 0, ROWS_DEV - 1).astype(jnp.int32)
    col_offset = place_ends(jax.random.randint(key_list[6], (SLOTS,), 0, COLS - PIX + 1), jax.random.fold_in(key_list[6], 1), 0, COLS - PIX).astype(jnp.int32)
    counts = draw_counts(jax.random.fold_in(key_list[8], 71), 0)
    return {"object_real": object_real, "object_imag": object_imag, "probe_real": probe_real, "probe_imag": probe_imag, "measured": measured, "row_offset": row_offset, "col_offset": col_offset, "counts": counts}


PROP_PHASE = 12.0
AMP_EPS = 0.05
OBJ_STEP = 1.0
PROBE_STEP = 4.0

def propagator(length):
    positions = jnp.arange(length, dtype=jnp.int32)
    frequency = ((positions + length // 2) % length - length // 2).astype(jnp.float32) / length
    phases = PROP_PHASE * (frequency[:, None] ** 2 + frequency[None, :] ** 2)
    return lax.complex(jnp.cos(phases), -jnp.sin(phases))

def tile_loss(strip_real, strip_imag, field_real, field_imag, row_start, col_start, measured_here, live_mask):
    kernel = propagator(PIX)
    anchor = jnp.int32(0)

    def cut_patch(row_here, col_here):
        begin = (anchor, row_here, col_here)
        return (lax.dynamic_slice(strip_real, begin, (SLICES, PIX, PIX)), lax.dynamic_slice(strip_imag, begin, (SLICES, PIX, PIX)))
    patch_real, patch_imag = jax.vmap(cut_patch)(row_start, col_start)
    patches = lax.complex(patch_real, patch_imag)
    wavefield = jnp.broadcast_to(lax.complex(field_real, field_imag)[None], (CAP, MODES, PIX, PIX))
    for level in range(SLICES):
        wavefield = wavefield * patches[:, level][:, None]
        if level < SLICES - 1:
            wavefield = jnp.fft.ifft2(kernel * jnp.fft.fft2(wavefield, norm='ortho'), norm='ortho')
    far_field = jnp.fft.fft2(wavefield, norm='ortho')
    intensity = lax.optimization_barrier(jnp.sum(jnp.real(far_field) ** 2 + jnp.imag(far_field) ** 2, axis=1))
    amplitude = jnp.sqrt(intensity + AMP_EPS)
    return 0.5 * jnp.sum(live_mask[:, None, None] * (amplitude - measured_here) ** 2)

def reference(object_real, object_imag, probe_real, probe_imag, measured, row_offset, col_offset, counts):
    wrap_real = jnp.concatenate([object_real, object_real[:, :PIX]], axis=1)
    wrap_imag = jnp.concatenate([object_imag, object_imag[:, :PIX]], axis=1)
    row_table = row_offset.reshape(N_TILE, CAP)
    col_table = col_offset.reshape(N_TILE, CAP)
    measured_table = measured.reshape(N_TILE, CAP, PIX, PIX)
    extent = ROWS_DEV + PIX

    def one_tile(carried, tile_idx):
        grad_real, grad_imag, probe_acc_real, probe_acc_imag = carried
        row_begin = tile_idx * ROWS_DEV
        strip_real = lax.dynamic_slice_in_dim(wrap_real, row_begin, extent, 1)
        strip_imag = lax.dynamic_slice_in_dim(wrap_imag, row_begin, extent, 1)
        live_mask = (jnp.arange(CAP, dtype=jnp.int32) < counts[tile_idx]).astype(object_real.dtype)
        rows_here = row_table[tile_idx]
        cols_here = col_table[tile_idx]
        measured_here = measured_table[tile_idx]

        def loss_of(part_real, part_imag, field_real, field_imag):
            return tile_loss(part_real, part_imag, field_real, field_imag, rows_here, cols_here, measured_here, live_mask)
        value, pullback = jax.vjp(loss_of, strip_real, strip_imag, probe_real, probe_imag)
        got_real, got_imag, got_probe_real, got_probe_imag = pullback(jnp.ones_like(value))
        grad_real = lax.dynamic_update_slice_in_dim(grad_real, lax.dynamic_slice_in_dim(grad_real, row_begin, extent, 1) + got_real, row_begin, 1)
        grad_imag = lax.dynamic_update_slice_in_dim(grad_imag, lax.dynamic_slice_in_dim(grad_imag, row_begin, extent, 1) + got_imag, row_begin, 1)
        return ((grad_real, grad_imag, probe_acc_real + got_probe_real, probe_acc_imag + got_probe_imag), None)
    initial = (jnp.zeros_like(wrap_real), jnp.zeros_like(wrap_imag), jnp.zeros_like(probe_real), jnp.zeros_like(probe_imag))
    (grad_real, grad_imag, probe_grad_real, probe_grad_imag), _ = lax.scan(one_tile, initial, jnp.arange(N_TILE, dtype=jnp.int32))
    total_real = jnp.concatenate([grad_real[:, :PIX] + grad_real[:, NROWS:], grad_real[:, PIX:NROWS]], axis=1)
    total_imag = jnp.concatenate([grad_imag[:, :PIX] + grad_imag[:, NROWS:], grad_imag[:, PIX:NROWS]], axis=1)
    live_total = jnp.sum(counts).astype(object_real.dtype)
    return (object_real - OBJ_STEP * total_real, object_imag - OBJ_STEP * total_imag, probe_real - PROBE_STEP * probe_grad_real / live_total, probe_imag - PROBE_STEP * probe_grad_imag / live_total)
```

```python
import jax
import jax.numpy as jnp
import numpy as np
from jax import lax
from jax.experimental import pallas as pl
from jax.experimental.pallas import tpu as pltpu
from jax.sharding import PartitionSpec as P

PIX = 128
SLICES = 12
GROUP = 3
PROP_PHASE = 12.0
AMP_EPS = 0.05
OBJ_STEP = 1.0
PROBE_STEP = 4.0


def split_const(matrix):
    high = matrix.astype(np.float32).astype(jnp.bfloat16)
    low = (matrix - high.astype(np.float64)).astype(np.float32).astype(jnp.bfloat16)
    return high, low


def make_constants():
    n = np.arange(PIX)
    dft = np.exp(-2j * np.pi * ((n[:, None] * n[None, :]) % PIX) / PIX) / np.sqrt(PIX)
    freq = ((n + PIX // 2) % PIX - PIX // 2) / PIX
    step = np.conj(dft) @ (np.exp(-1j * PROP_PHASE * freq**2)[:, None] * dft)
    out = []
    for matrix in (step, dft):
        real, imag = matrix.real, matrix.imag
        right = np.block([[real, imag], [-imag, real]])
        left = np.block([[real, -imag], [imag, real]])
        high, low = split_const(right)
        out.append(np.concatenate([high, high, low], axis=0))
        high, low = split_const(left)
        out.append(np.concatenate([high, high, low], axis=1))
    return out


def split(value):
    high = value.astype(jnp.bfloat16)
    low = (value - high.astype(jnp.float32)).astype(jnp.bfloat16)
    return high, low


def sandwich(field, right, left):
    wide = jnp.concatenate(
        [jnp.concatenate([field[0][m], field[1][m]], axis=1) for m in range(2)], axis=0
    )
    high, low = split(wide)
    middle = jnp.dot(
        jnp.concatenate([high, low, high], axis=1), right, preferred_element_type=jnp.float32
    )
    tall = jnp.concatenate(
        [
            jnp.concatenate([middle[:PIX, c * PIX : (c + 1) * PIX], middle[PIX:, c * PIX : (c + 1) * PIX]], axis=1)
            for c in range(2)
        ],
        axis=0,
    )
    high, low = split(tall)
    done = jnp.dot(
        left, jnp.concatenate([high, low, high], axis=0), preferred_element_type=jnp.float32
    )
    return [[done[c * PIX : (c + 1) * PIX, m * PIX : (m + 1) * PIX] for m in range(2)] for c in range(2)]


def times(patch_real, patch_imag, field):
    real = [field[0][m] * patch_real - field[1][m] * patch_imag for m in range(2)]
    imag = [field[0][m] * patch_imag + field[1][m] * patch_real for m in range(2)]
    return [real, imag]


def chain_kernel(
    live_ref, patch_ref, probe_real, probe_imag, measured_ref,
    step_right, step_left, dft_right, dft_left,
    piece_ref, probe_grad, waves,
):
    def load(ref, k):
        return [[ref[k, c, m] for m in range(2)] for c in range(2)]

    def store(ref, k, field):
        for c in range(2):
            for m in range(2):
                ref[k, c, m] = field[c][m]

    store(waves, 0, [[probe_real[m] for m in range(2)], [probe_imag[m] for m in range(2)]])

    def forward(k, carry):
        chi = times(patch_ref[k, 0], patch_ref[k, 1], load(waves, k))
        store(waves, k + 1, sandwich(chi, step_right[...], step_left[...]))
        return carry

    lax.fori_loop(0, SLICES - 1, forward, 0)
    last = SLICES - 1
    exit_wave = times(patch_ref[last, 0], patch_ref[last, 1], load(waves, last))
    far = sandwich(exit_wave, dft_right[...], dft_left[...])
    intensity = sum(far[c][m] * far[c][m] for c in range(2) for m in range(2))
    factor = (1.0 - measured_ref[...] * lax.rsqrt(intensity + AMP_EPS)) * live_ref[0]
    bent = [[far[0][m] * factor for m in range(2)], [-far[1][m] * factor for m in range(2)]]
    grad = sandwich(bent, dft_right[...], dft_left[...])

    def collect(k, grad):
        wave = load(waves, k)
        piece_ref[k, 0] = sum(wave[0][m] * grad[0][m] - wave[1][m] * grad[1][m] for m in range(2))
        piece_ref[k, 1] = -sum(wave[0][m] * grad[1][m] + wave[1][m] * grad[0][m] for m in range(2))
        return times(patch_ref[k, 0], patch_ref[k, 1], grad)

    store(waves, SLICES, grad)

    def backward(i, carry):
        k = last - i
        bent = collect(k, load(waves, SLICES))
        store(waves, SLICES, sandwich(bent, step_right[...], step_left[...]))
        return carry

    lax.fori_loop(0, SLICES - 1, backward, 0)
    entry = collect(0, load(waves, SLICES))
    for m in range(2):
        probe_grad[0, m] = entry[0][m]
        probe_grad[1, m] = -entry[1][m]


def run_chain(live, patches, probe_real, probe_imag, measured):
    vmem = pl.BlockSpec(memory_space=pltpu.VMEM)
    smem = pl.BlockSpec(memory_space=pltpu.SMEM)
    return pl.pallas_call(
        chain_kernel,
        out_shape=(
            jax.ShapeDtypeStruct((SLICES, 2, PIX, PIX), jnp.float32),
            jax.ShapeDtypeStruct((2, 2, PIX, PIX), jnp.float32),
        ),
        in_specs=[smem] + [vmem] * 8,
        out_specs=(vmem, vmem),
        scratch_shapes=[pltpu.VMEM((SLICES + 1, 2, 2, PIX, PIX), jnp.float32)],
        compiler_params=pltpu.CompilerParams(vmem_limit_bytes=40 * 1024 * 1024),
    )(live, patches, probe_real, probe_imag, measured, *[jnp.asarray(c) for c in make_constants()])


def shifted(block, axis, distance):
    count = lax.axis_size(axis)
    return lax.ppermute(block, axis, [((i - distance) % count, i) for i in range(count)])


def body(
    object_real, object_imag, probe_real, probe_imag, measured, row_offset, col_offset, counts
):
    slices_dev, rows_dev, _ = object_real.shape
    slot_count = row_offset.shape[0]
    depth_index = lax.axis_index("depth")
    depth_count = lax.axis_size("depth")
    objects = jnp.stack([object_real, object_imag], axis=1)
    extended = jnp.concatenate([objects, shifted(objects, "tile", -1)], axis=2)
    patches = jnp.stack(
        [
            lax.dynamic_slice(extended, (0, 0, row_offset[s], col_offset[s]), (slices_dev, 2, PIX, PIX))
            for s in range(slot_count)
        ]
    )
    mine = lax.all_to_all(patches, "depth", 0, 0, tiled=True).reshape(SLICES, 2, PIX, PIX)
    own_count = lax.dynamic_index_in_dim(counts, lax.axis_index("tile"), 0, keepdims=False)
    live = (depth_index < own_count).astype(jnp.float32).reshape(1)
    own_measured = lax.dynamic_index_in_dim(measured, depth_index, 0, keepdims=False)
    pieces, probe_grad = run_chain(live, mine, probe_real, probe_imag, own_measured)
    back = lax.all_to_all(
        pieces.reshape(depth_count, slices_dev, 2, PIX, PIX), "depth", 0, 0, tiled=True
    )
    total = jnp.zeros_like(extended)
    for s in range(slot_count):
        start = (0, 0, row_offset[s], col_offset[s])
        block = lax.dynamic_slice(total, start, (slices_dev, 2, PIX, PIX))
        total = lax.dynamic_update_slice(total, block + back[s], start)
    object_grad = total[:, :, :rows_dev] + shifted(total[:, :, rows_dev:], "tile", 1)
    rows = PIX // depth_count
    grad_mine = lax.psum_scatter(probe_grad, "depth", scatter_dimension=2, tiled=True)
    grad_mine = lax.psum(grad_mine, "tile")
    real_mine = lax.dynamic_slice_in_dim(probe_real, depth_index * rows, rows, 1)
    imag_mine = lax.dynamic_slice_in_dim(probe_imag, depth_index * rows, rows, 1)
    live_total = jnp.sum(counts).astype(jnp.float32)
    return (
        object_real - OBJ_STEP * object_grad[:, 0],
        object_imag - OBJ_STEP * object_grad[:, 1],
        real_mine - PROBE_STEP * grad_mine[0] / live_total,
        imag_mine - PROBE_STEP * grad_mine[1] / live_total,
    )


def solution(mesh):
    placed = (
        P("depth", "tile", None),
        P("depth", "tile", None),
        P(),
        P(),
        P("tile", None, None),
        P("tile"),
        P("tile"),
        P(),
    )
    return jax.shard_map(
        body,
        mesh=mesh,
        in_specs=placed,
        out_specs=(
            P("depth", "tile", None),
            P("depth", "tile", None),
            P(None, "depth", None),
            P(None, "depth", None),
        ),
        check_vma=False,
    )
```

```python
import functools

import jax
import jax.numpy as jnp
import numpy as np
from jax import lax
from jax.experimental import pallas as pl
from jax.experimental.pallas import tpu as pltpu
from jax.sharding import PartitionSpec as P

PIX = 128
SLICES = 12
GROUP = 3
RING = 16
PROP_PHASE = 12.0
AMP_EPS = 0.05
OBJ_STEP = 1.0
PROBE_STEP = 4.0


def split_const(matrix):
    high = matrix.astype(np.float32).astype(jnp.bfloat16)
    low = (matrix - high.astype(np.float64)).astype(np.float32).astype(jnp.bfloat16)
    return high, low


def make_constants():
    n = np.arange(PIX)
    dft = np.exp(-2j * np.pi * ((n[:, None] * n[None, :]) % PIX) / PIX) / np.sqrt(PIX)
    freq = ((n + PIX // 2) % PIX - PIX // 2) / PIX
    step = np.conj(dft) @ (np.exp(-1j * PROP_PHASE * freq**2)[:, None] * dft)
    out = []
    for matrix in (step, dft):
        real, imag = matrix.real, matrix.imag
        right = np.block([[real, imag], [-imag, real]])
        left = np.block([[real, -imag], [imag, real]])
        high, low = split_const(right)
        out.append(np.concatenate([high, high, low], axis=0))
        high, low = split_const(left)
        out.append(np.concatenate([high, high, low], axis=1))
    return out


def split(value):
    high = value.astype(jnp.bfloat16)
    low = (value - high.astype(jnp.float32)).astype(jnp.bfloat16)
    return high, low


def sandwich(field, right, left):
    wide = jnp.concatenate(
        [jnp.concatenate([field[0][m], field[1][m]], axis=1) for m in range(2)], axis=0
    )
    high, low = split(wide)
    middle = jnp.dot(
        jnp.concatenate([high, low, high], axis=1), right, preferred_element_type=jnp.float32
    )
    tall = jnp.concatenate(
        [
            jnp.concatenate([middle[:PIX, c * PIX : (c + 1) * PIX], middle[PIX:, c * PIX : (c + 1) * PIX]], axis=1)
            for c in range(2)
        ],
        axis=0,
    )
    high, low = split(tall)
    done = jnp.dot(
        left, jnp.concatenate([high, low, high], axis=0), preferred_element_type=jnp.float32
    )
    return [[done[c * PIX : (c + 1) * PIX, m * PIX : (m + 1) * PIX] for m in range(2)] for c in range(2)]


def times(patch_real, patch_imag, field):
    real = [field[0][m] * patch_real - field[1][m] * patch_imag for m in range(2)]
    imag = [field[0][m] * patch_imag + field[1][m] * patch_real for m in range(2)]
    return [real, imag]


MESH = pl.DeviceIdType.MESH


def turned(block, rows, cols):
    return pltpu.roll(pltpu.roll(block, rows, 0), cols, 1)


def kernel(
    n_tile, n_depth, ring,
    row_ref, col_ref, count_ref, obj_real, obj_imag, probe_real, probe_imag, measured_ref,
    step_right, step_left, dft_right, dft_left,
    new_real, new_imag, new_probe_real, new_probe_imag,
    head, stage, patch_ref, waves, piece_stage, grads, own_sum, next_sum, next_recv,
    parts, parts_recv, line, line_recv, cross_recv, final,
    head_send_sem, head_recv_sem, patch_send_sem, patch_recv_sem, piece_send_sem, grad_recv_sem,
    next_send_sem, next_recv_sem, part_send_sem, part_recv_sem, line_send_sem, line_recv_sem,
    cross_send_sem, cross_recv_sem, final_send_sem, final_recv_sem,
):
    objects = (obj_real, obj_imag)
    tile = lax.axis_index("tile")
    depth = lax.axis_index("depth")
    after, before = lax.rem(tile + 1, n_tile), lax.rem(tile + n_tile - 1, n_tile)
    n_line = n_tile // ring
    spot, row_of = lax.rem(tile, ring), tile // ring
    ring_base = row_of * ring

    def send(src, dst, send_sem, recv_sem, to_tile, to_depth):
        return pltpu.make_async_remote_copy(
            src_ref=src, dst_ref=dst, send_sem=send_sem, recv_sem=recv_sem,
            device_id=(to_tile, to_depth), device_id_type=MESH,
        )

    def ring_peer(i):
        return lax.rem(spot + i, ring)

    def line_peer(i):
        return lax.rem(row_of + i, n_line)

    def depth_peer(i):
        return lax.rem(depth + i, n_depth)

    barrier = pltpu.get_barrier_semaphore()

    def greet(to_tile, to_depth):
        pl.semaphore_signal(barrier, inc=1, device_id=(to_tile, to_depth), device_id_type=MESH)

    greet(after, depth)
    greet(before, depth)
    lax.fori_loop(1, n_depth, lambda i, c: (greet(tile, depth_peer(i)), c)[1], 0)
    lax.fori_loop(1, ring, lambda i, c: (greet(ring_base + ring_peer(i), depth), c)[1], 0)
    lax.fori_loop(1, n_line, lambda i, c: (greet(line_peer(i) * ring + spot, depth), c)[1], 0)
    pl.semaphore_wait(barrier, 2 + n_depth - 1 + ring - 1 + n_line - 1)

    def head_copy(j, c):
        return send(objects[c].at[j], head.at[j, c], head_send_sem.at[j, c], head_recv_sem.at[j, c], before, depth)

    for j in range(GROUP):
        for c in range(2):
            head_copy(j, c).start()

    row_iota = lax.broadcasted_iota(jnp.int32, (PIX, PIX), 0)
    col_iota = lax.broadcasted_iota(jnp.int32, (PIX, PIX), 1)

    def patch_copy(j, to_depth):
        k = depth * GROUP + j
        return send(
            stage.at[j, to_depth], patch_ref.at[k],
            patch_send_sem.at[j, to_depth], patch_recv_sem.at[k], tile, to_depth,
        )

    def cut(j, i):
        slot = depth_peer(i)
        row, col = row_ref[slot], col_ref[slot]
        own_row, left_col = row_iota >= row, col_iota >= col
        out = []
        for c in range(2):
            upper = jnp.where(left_col, objects[c][j, :, :PIX], objects[c][j, :, PIX:])
            lower = jnp.where(left_col, head[j, c, :, :PIX], head[j, c, :, PIX:])
            block = jnp.where(own_row, upper, lower)
            out.append(turned(block, lax.rem(PIX - row, PIX), lax.rem(PIX - col + PIX, PIX)))
        return slot, out

    def cut_slice(j, carry):
        for c in range(2):
            send(objects[0].at[j], head.at[j, c], head_send_sem.at[j, c], head_recv_sem.at[j, c], before, depth).wait_recv()

        def cut_slot(i, carry):
            slot, out = cut(j, i)
            for c in range(2):
                stage[j, slot, c] = out[c]
            patch_copy(j, slot).start()
            return carry

        lax.fori_loop(1, n_depth, cut_slot, 0)
        _, out = cut(j, 0)
        for c in range(2):
            patch_ref[depth * GROUP + j, c] = out[c]
        return carry

    lax.fori_loop(0, GROUP, cut_slice, 0)

    def load(ref, k):
        return [[ref[k, c, m] for m in range(2)] for c in range(2)]

    def store(ref, k, field):
        for c in range(2):
            for m in range(2):
                ref[k, c, m] = field[c][m]

    def patch_ready(k):
        @pl.when(k // GROUP != depth)
        def _():
            send(stage.at[0, 0], patch_ref.at[k], patch_send_sem.at[0, 0], patch_recv_sem.at[k], tile, depth).wait_recv()

    store(waves, 0, [[probe_real[m] for m in range(2)], [probe_imag[m] for m in range(2)]])

    def forward(k, carry):
        patch_ready(k)
        chi = times(patch_ref[k, 0], patch_ref[k, 1], load(waves, k))
        store(waves, k + 1, sandwich(chi, step_right[...], step_left[...]))
        return carry

    last = SLICES - 1
    lax.fori_loop(0, last, forward, 0)
    patch_ready(last)
    exit_wave = times(patch_ref[last, 0], patch_ref[last, 1], load(waves, last))
    far = sandwich(exit_wave, dft_right[...], dft_left[...])
    intensity = sum(far[c][m] * far[c][m] for c in range(2) for m in range(2))
    live = jnp.where(depth < count_ref[tile], 1.0, 0.0)
    factor = (1.0 - measured_ref[depth] * lax.rsqrt(intensity + AMP_EPS)) * live
    bent = [[far[0][m] * factor for m in range(2)], [-far[1][m] * factor for m in range(2)]]
    store(waves, SLICES, sandwich(bent, dft_right[...], dft_left[...]))

    own_turn = (row_ref[depth], col_ref[depth])

    def collect(k, grad):
        wave = load(waves, k)
        real = sum(wave[0][m] * grad[0][m] - wave[1][m] * grad[1][m] for m in range(2))
        imag = -sum(wave[0][m] * grad[1][m] + wave[1][m] * grad[0][m] for m in range(2))
        row, col = own_turn
        piece_stage[k, 0] = turned(real, row, lax.rem(col, PIX))
        piece_stage[k, 1] = turned(imag, row, lax.rem(col, PIX))
        return times(patch_ref[k, 0], patch_ref[k, 1], grad)

    def piece_copy(k):
        return send(
            piece_stage.at[k], grads.at[lax.rem(k, GROUP), depth],
            piece_send_sem.at[k], grad_recv_sem.at[lax.rem(k, GROUP), depth], tile, k // GROUP,
        )

    def deliver(k):
        @pl.when(k // GROUP != depth)
        def _():
            piece_copy(k).start()

        @pl.when(k // GROUP == depth)
        def _():
            grads[lax.rem(k, GROUP), depth] = piece_stage[k]

    def backward(i, carry):
        k = last - i
        bent = collect(k, load(waves, SLICES))
        store(waves, SLICES, sandwich(bent, step_right[...], step_left[...]))
        deliver(k)
        return carry

    lax.fori_loop(0, last, backward, 0)
    entry = collect(0, load(waves, SLICES))
    deliver(0)

    quarter = PIX // n_depth
    height = 4 * quarter // ring
    for c in range(2):
        for m in range(2):
            value = entry[c][m] if c == 0 else -entry[c][m]
            for d in range(n_depth):
                for i in range(0, quarter, 8):
                    flat = (c * 2 + m) * quarter + i
                    parts[flat // height, d, flat % height : flat % height + 8] = value[
                        d * quarter + i : d * quarter + i + 8
                    ]

    def part_copy(i):
        to = ring_peer(i)
        return send(
            parts.at[to], parts_recv.at[spot], part_send_sem.at[to], part_recv_sem.at[spot],
            ring_base + to, depth,
        )

    def line_copy(i):
        to = line_peer(i)
        return send(
            line, line_recv.at[row_of], line_send_sem.at[to], line_recv_sem.at[row_of],
            to * ring + spot, depth,
        )

    def cross_copy(i):
        to = depth_peer(i)
        return send(
            line_recv.at[n_line, to], cross_recv.at[depth], cross_send_sem.at[to], cross_recv_sem.at[depth],
            tile, to,
        )

    def final_copy(i):
        to = ring_peer(i)
        return send(
            cross_recv.at[n_depth], final.at[spot], final_send_sem.at[to], final_recv_sem.at[spot],
            ring_base + to, depth,
        )

    def start_all(copy, count):
        lax.fori_loop(1, count, lambda i, c: (copy(i).start(), c)[1], 0)

    def wait_sent(copy, count):
        lax.fori_loop(1, count, lambda i, c: (copy(i).wait_send(), c)[1], 0)

    def wait_got(buffer, send_sem, recv_sem, peer, count):
        def one(i, carry):
            frm = peer(i)
            send(buffer.at[frm], buffer.at[frm], send_sem.at[frm], recv_sem.at[frm], tile, depth).wait_recv()
            return carry

        lax.fori_loop(1, count, one, 0)

    parts_recv[spot] = parts[spot]
    start_all(part_copy, ring)

    def next_copy(j):
        return send(next_sum.at[j], next_recv.at[j], next_send_sem.at[j], next_recv_sem.at[j], after, depth)

    def gather_slice(j):
        def arrived(i, carry):
            frm = depth_peer(i)
            send(grads.at[j, frm], grads.at[j, frm], grad_recv_sem.at[j, frm], grad_recv_sem.at[j, frm], tile, depth).wait_recv()
            return carry

        lax.fori_loop(1, n_depth, arrived, 0)
        for c in range(2):
            sums = [0.0] * 4
            for slot in range(n_depth):
                own_row, left_col = row_iota >= row_ref[slot], col_iota >= col_ref[slot]
                block = grads[j, slot, c]
                upper = jnp.where(own_row, block, 0.0)
                lower = block - upper
                upper_left = jnp.where(left_col, upper, 0.0)
                lower_left = jnp.where(left_col, lower, 0.0)
                terms = (upper_left, upper - upper_left, lower_left, lower - lower_left)
                sums = [a + b for a, b in zip(sums, terms)]
            own_sum[j, c, :, :PIX] = sums[0]
            own_sum[j, c, :, PIX:] = sums[1]
            next_sum[j, c, :, :PIX] = sums[2]
            next_sum[j, c, :, PIX:] = sums[3]
        next_copy(j).start()

    def finish_slice(j):
        next_copy(j).wait_recv()
        for c, target in ((0, new_real), (1, new_imag)):
            target[j] = objects[c][j] - OBJ_STEP * (own_sum[j, c] + next_recv[j, c])

    gather_slice(2)

    wait_got(parts_recv, part_send_sem, part_recv_sem, ring_peer, ring)
    total = parts_recv[0]
    for i in range(1, ring):
        total = total + parts_recv[i]
    line[...] = total
    line_recv[row_of] = total
    start_all(line_copy, n_line)

    gather_slice(1)

    wait_got(line_recv, line_send_sem, line_recv_sem, line_peer, n_line)
    total = line_recv[0]
    for i in range(1, n_line):
        total = total + line_recv[i]
    line_recv[n_line] = total
    cross_recv[depth] = line_recv[n_line, depth]
    start_all(cross_copy, n_depth)
    wait_got(cross_recv, cross_send_sem, cross_recv_sem, depth_peer, n_depth)
    total = cross_recv[0]
    for i in range(1, n_depth):
        total = total + cross_recv[i]
    cross_recv[n_depth] = total
    final[spot] = total
    start_all(final_copy, ring)

    gather_slice(0)
    finish_slice(2)
    finish_slice(1)
    wait_got(final, final_send_sem, final_recv_sem, ring_peer, ring)
    live_total = lax.fori_loop(0, n_tile, lambda i, acc: acc + count_ref[i], 0).astype(jnp.float32)
    rows = pl.ds(pl.multiple_of(depth * quarter, quarter), quarter)
    for c, source, target in ((0, probe_real, new_probe_real), (1, probe_imag, new_probe_imag)):
        for m in range(2):
            for i in range(0, quarter, 8):
                flat = (c * 2 + m) * quarter + i
                grad = final[flat // height, flat % height : flat % height + 8]
                start = pl.multiple_of(depth * quarter + i, 8)
                target[m, i : i + 8] = source[m, pl.ds(start, 8)] - PROBE_STEP * grad / live_total
    finish_slice(0)

    for j in range(GROUP):
        for c in range(2):
            head_copy(j, c).wait_send()
        lax.fori_loop(1, n_depth, lambda i, c, j=j: (patch_copy(j, depth_peer(i)).wait_send(), c)[1], 0)
        next_copy(j).wait_send()

    def piece_sent(k, carry):
        @pl.when(k // GROUP != depth)
        def _():
            piece_copy(k).wait_send()

        return carry

    lax.fori_loop(0, SLICES, piece_sent, 0)
    wait_sent(part_copy, ring)
    wait_sent(line_copy, n_line)
    wait_sent(cross_copy, n_depth)
    wait_sent(final_copy, ring)


def body(
    object_real, object_imag, probe_real, probe_imag, measured, row_offset, col_offset, counts
):
    n_tile, n_depth = lax.axis_size("tile"), lax.axis_size("depth")
    ring = RING if n_tile % RING == 0 else 2
    n_line = n_tile // ring
    slab = object_real.shape
    cols = slab[2]
    height = PIX // ring
    vmem = pl.BlockSpec(memory_space=pltpu.VMEM)
    smem = pl.BlockSpec(memory_space=pltpu.SMEM)
    f32 = jnp.float32
    dma = pltpu.SemaphoreType.DMA
    return pl.pallas_call(
        functools.partial(kernel, n_tile, n_depth, ring),
        out_shape=(
            jax.ShapeDtypeStruct(slab, f32),
            jax.ShapeDtypeStruct(slab, f32),
            jax.ShapeDtypeStruct((2, PIX // n_depth, PIX), f32),
            jax.ShapeDtypeStruct((2, PIX // n_depth, PIX), f32),
        ),
        in_specs=[smem] * 3 + [vmem] * 9,
        out_specs=(vmem,) * 4,
        scratch_shapes=[
            pltpu.VMEM((GROUP, 2, PIX, cols), f32),
            pltpu.VMEM((GROUP, n_depth, 2, PIX, PIX), f32),
            pltpu.VMEM((SLICES, 2, PIX, PIX), f32),
            pltpu.VMEM((SLICES + 1, 2, 2, PIX, PIX), f32),
            pltpu.VMEM((SLICES, 2, PIX, PIX), f32),
            pltpu.VMEM((GROUP, n_depth, 2, PIX, PIX), f32),
            pltpu.VMEM((GROUP, 2, PIX, cols), f32),
            pltpu.VMEM((GROUP, 2, PIX, cols), f32),
            pltpu.VMEM((GROUP, 2, PIX, cols), f32),
            pltpu.VMEM((ring, n_depth, height, PIX), f32),
            pltpu.VMEM((ring, n_depth, height, PIX), f32),
            pltpu.VMEM((n_depth, height, PIX), f32),
            pltpu.VMEM((n_line + 1, n_depth, height, PIX), f32),
            pltpu.VMEM((n_depth + 1, height, PIX), f32),
            pltpu.VMEM((ring, height, PIX), f32),
            dma((GROUP, 2)), dma((GROUP, 2)), dma((GROUP, n_depth)), dma((SLICES,)),
            dma((SLICES,)), dma((GROUP, n_depth)), dma((GROUP,)), dma((GROUP,)),
            dma((ring,)), dma((ring,)), dma((n_line,)), dma((n_line,)),
            dma((n_depth,)), dma((n_depth,)), dma((ring,)), dma((ring,)),
        ],
        compiler_params=pltpu.CompilerParams(
            collective_id=0, has_side_effects=True, vmem_limit_bytes=44 * 1024 * 1024
        ),
    )(
        row_offset, col_offset, counts, object_real, object_imag, probe_real, probe_imag, measured,
        *[jnp.asarray(c) for c in make_constants()],
    )


def solution(mesh):
    placed = (
        P("depth", "tile", None),
        P("depth", "tile", None),
        P(),
        P(),
        P("tile", None, None),
        P("tile"),
        P("tile"),
        P(),
    )
    return jax.shard_map(
        body,
        mesh=mesh,
        in_specs=placed,
        out_specs=(
            P("depth", "tile", None),
            P("depth", "tile", None),
            P(None, "depth", None),
            P(None, "depth", None),
        ),
        check_vma=False,
    )
```

```python
import functools

import jax
import jax.numpy as jnp
import numpy as np
from jax import lax
from jax.experimental import pallas as pl
from jax.experimental.pallas import tpu as pltpu
from jax.sharding import PartitionSpec as P

PIX = 128
SLICES = 12
GROUP = 3
RING = 16
PROP_PHASE = 12.0
AMP_EPS = 0.05
OBJ_STEP = 1.0
PROBE_STEP = 4.0


def make_constants():
    n = np.arange(PIX)
    dft = np.exp(-2j * np.pi * ((n[:, None] * n[None, :]) % PIX) / PIX) / np.sqrt(PIX)
    freq = ((n + PIX // 2) % PIX - PIX // 2) / PIX
    step = np.conj(dft) @ (np.exp(-1j * PROP_PHASE * freq**2)[:, None] * dft)
    return np.stack([step.real, step.imag, dft.real, dft.imag]).astype(np.float32)


def split(value):
    high = value.astype(jnp.bfloat16)
    low = (value - high.astype(jnp.float32)).astype(jnp.bfloat16)
    return high, low


def make_factors(real, imag, right, left):
    for i, line in enumerate(((real, imag), (-imag, real))):
        high, low = split(jnp.concatenate(line, axis=1))
        for n, part in enumerate((high, high, low)):
            right[2 * n * PIX + i * PIX : 2 * n * PIX + (i + 1) * PIX] = part
    for i, line in enumerate(((real, -imag), (imag, real))):
        high, low = split(jnp.concatenate(line, axis=1))
        for n, part in enumerate((high, high, low)):
            left[i * PIX : (i + 1) * PIX, 2 * n * PIX : 2 * (n + 1) * PIX] = part


def sandwich(field, right, left):
    wide = jnp.concatenate(
        [jnp.concatenate([field[0][m], field[1][m]], axis=1) for m in range(2)], axis=0
    )
    high, low = split(wide)
    middle = jnp.dot(
        jnp.concatenate([high, low, high], axis=1), right, preferred_element_type=jnp.float32
    )
    tall = jnp.concatenate(
        [
            jnp.concatenate([middle[:PIX, c * PIX : (c + 1) * PIX], middle[PIX:, c * PIX : (c + 1) * PIX]], axis=1)
            for c in range(2)
        ],
        axis=0,
    )
    high, low = split(tall)
    done = jnp.dot(
        left, jnp.concatenate([high, low, high], axis=0), preferred_element_type=jnp.float32
    )
    return [[done[c * PIX : (c + 1) * PIX, m * PIX : (m + 1) * PIX] for m in range(2)] for c in range(2)]


def times(patch_real, patch_imag, field):
    real = [field[0][m] * patch_real - field[1][m] * patch_imag for m in range(2)]
    imag = [field[0][m] * patch_imag + field[1][m] * patch_real for m in range(2)]
    return [real, imag]


MESH = pl.DeviceIdType.MESH


def turned(block, rows, cols):
    return pltpu.roll(pltpu.roll(block, rows, 0), cols, 1)


def kernel(
    n_tile, n_depth, ring,
    row_hbm, col_hbm, count_hbm, real_hbm, imag_hbm, probe_real_hbm, probe_imag_hbm, measured_hbm,
    table_hbm,
    new_real, new_imag, new_probe_real, new_probe_imag,
    head, stage, patch_ref, waves, piece_stage, grads, own_sum, next_sum, next_recv,
    parts, core_recv, column, column_recv, plane, plane_recv, final,
    row_ref, col_ref, count_ref, obj_real, obj_imag, probe_real, probe_imag, measured_ref,
    step_right, step_left, dft_right, dft_left, table, load_sem, new_probe, store_sem,
    head_send_sem, head_recv_sem, patch_send_sem, patch_recv_sem, piece_send_sem, grad_recv_sem,
    next_send_sem, next_recv_sem,
    core_sem, column_send_sem, column_recv_sem, plane_send_sem, plane_recv_sem, final_send_sem, final_recv_sem,
):
    objects = (obj_real, obj_imag)
    sources = (real_hbm, imag_hbm)
    tile = lax.axis_index("tile")
    depth = lax.axis_index("depth")

    def fetch(n, src, dst):
        copy = pltpu.make_async_copy(src, dst, load_sem.at[n])
        copy.start()
        return copy

    offset_loads = [fetch(0, row_hbm, row_ref), fetch(1, col_hbm, col_ref)]
    object_loads = [fetch(2, real_hbm, obj_real), fetch(3, imag_hbm, obj_imag)]
    probe_loads = [fetch(4, probe_real_hbm, probe_real), fetch(5, probe_imag_hbm, probe_imag)]
    table_loads = [fetch(6, table_hbm, table)]
    far_loads = [fetch(7, measured_hbm.at[depth], measured_ref), fetch(8, count_hbm, count_ref)]

    def loaded(copies):
        for copy in copies:
            copy.wait()

    after, before = lax.rem(tile + 1, n_tile), lax.rem(tile + n_tile - 1, n_tile)
    n_line = n_tile // ring
    spot, row_of = lax.rem(tile, ring), tile // ring
    ring_base = row_of * ring

    def send(src, dst, send_sem, recv_sem, to_tile, to_depth):
        return pltpu.make_async_remote_copy(
            src_ref=src, dst_ref=dst, send_sem=send_sem, recv_sem=recv_sem,
            device_id=(to_tile, to_depth), device_id_type=MESH,
        )

    def ring_peer(i):
        return lax.rem(spot + i, ring)

    plane_spot = row_of * n_depth + depth

    def plane_peer(i):
        return lax.rem(plane_spot + i, n_line * n_depth)

    def plane_device(n):
        return (n // n_depth) * ring + spot, lax.rem(n, n_depth)

    core, column_spot, n_column = lax.rem(spot, 2), spot // 2, ring // 2

    def column_peer(i):
        return lax.rem(column_spot + i, n_column)

    def depth_peer(i):
        return lax.rem(depth + i, n_depth)

    barrier = pltpu.get_barrier_semaphore()

    def greet(to_tile, to_depth):
        pl.semaphore_signal(barrier, inc=1, device_id=(to_tile, to_depth), device_id_type=MESH)

    greet(after, depth)
    greet(before, depth)
    lax.fori_loop(1, ring, lambda i, c: (greet(ring_base + ring_peer(i), depth), c)[1], 0)
    lax.fori_loop(1, n_line * n_depth, lambda i, c: (greet(*plane_device(plane_peer(i))), c)[1], 0)
    pl.semaphore_wait(barrier, 2 + ring - 1 + n_line * n_depth - 1)

    def head_copy(j, c):
        return send(sources[c].at[j], head.at[j, c], head_send_sem.at[j, c], head_recv_sem.at[j, c], before, depth)

    def start_head(j):
        for c in range(2):
            head_copy(j, c).start()

    start_head(0)

    row_iota = lax.broadcasted_iota(jnp.int32, (PIX, PIX), 0)
    col_iota = lax.broadcasted_iota(jnp.int32, (PIX, PIX), 1)

    def patch_copy(j, to):
        k = depth * GROUP + j
        return send(
            stage.at[j, to], patch_ref.at[k], patch_send_sem.at[j, to], patch_recv_sem.at[k], tile, to
        )

    def each_patch_send(j, act):
        for i in (2, 1, 3):
            act(patch_copy(j, depth_peer(i)))

    def start(copy):
        copy.start()

    def wait_send(copy):
        copy.wait_send()

    def cut(j, i):
        slot = depth_peer(i)
        row, col = row_ref[slot], col_ref[slot]
        own_row, left_col = row_iota >= row, col_iota >= col
        out = []
        for c in range(2):
            upper = jnp.where(left_col, objects[c][j, :, :PIX], objects[c][j, :, PIX:])
            lower = jnp.where(left_col, head[j, c, :, :PIX], head[j, c, :, PIX:])
            block = jnp.where(own_row, upper, lower)
            out.append(turned(block, lax.rem(PIX - row, PIX), lax.rem(PIX - col + PIX, PIX)))
        return slot, out

    def cut_slice(j, carry):
        for c in range(2):
            head_copy(j, c).wait_recv()

        @pl.when(j + 1 < GROUP)
        def _():
            start_head(j + 1)

        def cut_slot(i, carry):
            slot, out = cut(j, i)
            for c in range(2):
                stage[j, slot, c] = out[c]
            return carry

        lax.fori_loop(1, n_depth, cut_slot, 0)

        each_patch_send(j, start)
        _, out = cut(j, 0)
        for c in range(2):
            patch_ref[depth * GROUP + j, c] = out[c]
        return carry

    loaded(offset_loads)
    loaded(object_loads)
    lax.fori_loop(0, GROUP, cut_slice, 0)

    def load(ref, k):
        return [[ref[k, c, m] for m in range(2)] for c in range(2)]

    def store(ref, k, field):
        for c in range(2):
            for m in range(2):
                ref[k, c, m] = field[c][m]

    def patch_ready(k):
        @pl.when(k // GROUP != depth)
        def _():
            send(stage.at[0, 0], patch_ref.at[k], patch_send_sem.at[0, 0], patch_recv_sem.at[k], tile, depth).wait_recv()

    loaded(probe_loads)
    loaded(table_loads)
    make_factors(table[0], table[1], step_right, step_left)
    make_factors(table[2], table[3], dft_right, dft_left)
    store(waves, 0, [[probe_real[m] for m in range(2)], [probe_imag[m] for m in range(2)]])

    def forward(k, carry):
        patch_ready(k)

        chi = times(patch_ref[k, 0], patch_ref[k, 1], load(waves, k))
        store(waves, k + 1, sandwich(chi, step_right[...], step_left[...]))
        return carry

    last = SLICES - 1
    lax.fori_loop(0, last, forward, 0)
    patch_ready(last)
    loaded(far_loads)
    exit_wave = times(patch_ref[last, 0], patch_ref[last, 1], load(waves, last))
    far = sandwich(exit_wave, dft_right[...], dft_left[...])
    intensity = sum(far[c][m] * far[c][m] for c in range(2) for m in range(2))
    live = jnp.where(depth < count_ref[tile], 1.0, 0.0)
    factor = (1.0 - measured_ref[...] * lax.rsqrt(intensity + AMP_EPS)) * live
    bent = [[far[0][m] * factor for m in range(2)], [-far[1][m] * factor for m in range(2)]]
    store(waves, SLICES, sandwich(bent, dft_right[...], dft_left[...]))

    own_turn = (row_ref[depth], col_ref[depth])

    def collect(k, grad):
        wave = load(waves, k)
        real = sum(wave[0][m] * grad[0][m] - wave[1][m] * grad[1][m] for m in range(2))
        imag = -sum(wave[0][m] * grad[1][m] + wave[1][m] * grad[0][m] for m in range(2))
        row, col = own_turn
        piece_stage[k, 0] = turned(real, row, lax.rem(col, PIX))
        piece_stage[k, 1] = turned(imag, row, lax.rem(col, PIX))
        return times(patch_ref[k, 0], patch_ref[k, 1], grad)

    def piece_copy(k):
        j = lax.rem(k, GROUP)
        return send(
            piece_stage.at[k], grads.at[j, depth], piece_send_sem.at[k], grad_recv_sem.at[j, depth], tile, k // GROUP
        )

    def deliver(k):
        here = k // GROUP == depth

        @pl.when(jnp.logical_and(jnp.logical_not(here), k > 1))
        def _():
            piece_copy(k).start()

        @pl.when(here)
        def _():
            grads[lax.rem(k, GROUP), depth] = piece_stage[k]

    def release(k):
        @pl.when(depth != 0)
        def _():
            piece_copy(k + 1).wait_send()
            piece_copy(k).start()

    def backward(i, carry):
        k = last - i
        bent = collect(k, load(waves, SLICES))
        store(waves, SLICES, sandwich(bent, step_right[...], step_left[...]))
        deliver(k)
        return carry

    lax.fori_loop(0, last, backward, 0)
    entry = collect(0, load(waves, SLICES))
    deliver(0)

    quarter = PIX // n_depth
    height = 4 * quarter // ring
    for c in range(2):
        for m in range(2):
            value = entry[c][m] if c == 0 else -entry[c][m]
            for d in range(n_depth):
                for i in range(0, quarter, 8):
                    flat = (c * 2 + m) * quarter + i
                    part = flat // height
                    parts[part % 2, part // 2, d, flat % height : flat % height + 8] = value[
                        d * quarter + i : d * quarter + i + 8
                    ]

    core_copy = send(parts.at[1 - core], core_recv, core_sem.at[0], core_sem.at[1], tile + 1 - 2 * core, depth)

    def column_copy(i):
        to = column_peer(i)
        return send(
            column.at[to], column_recv.at[column_spot], column_send_sem.at[to], column_recv_sem.at[column_spot],
            ring_base + 2 * to + core, depth,
        )

    def plane_copy(i):
        to = plane_peer(i)
        to_tile, to_depth = plane_device(to)
        return send(
            plane.at[to_depth], plane_recv.at[plane_spot], plane_send_sem.at[to], plane_recv_sem.at[plane_spot],
            to_tile, to_depth,
        )

    def final_copy(i):
        to = ring_peer(i)
        return send(
            final.at[spot], final.at[spot], final_send_sem.at[to], final_recv_sem.at[spot],
            ring_base + to, depth,
        )

    def start_all(copy, count):
        lax.fori_loop(1, count, lambda i, c: (copy(i).start(), c)[1], 0)

    def wait_sent(copy, count):
        lax.fori_loop(1, count, lambda i, c: (copy(i).wait_send(), c)[1], 0)

    def wait_got(buffer, send_sem, recv_sem, peer, count):
        def one(i, carry):
            frm = peer(i)
            send(buffer.at[frm], buffer.at[frm], send_sem.at[frm], recv_sem.at[frm], tile, depth).wait_recv()
            return carry

        lax.fori_loop(1, count, one, 0)

    def next_copy(j):
        return send(next_sum.at[j], next_recv.at[j], next_send_sem.at[j], next_recv_sem.at[j], after, depth)

    def gather_slice(j):
        def arrived(i, carry):
            frm = depth_peer(i)
            sem = grad_recv_sem.at[j, frm]
            send(grads.at[j, frm], grads.at[j, frm], sem, sem, tile, depth).wait_recv()
            return carry

        lax.fori_loop(1, n_depth, arrived, 0)
        for c in range(2):
            sums = [0.0] * 4
            for slot in range(n_depth):
                own_row, left_col = row_iota >= row_ref[slot], col_iota >= col_ref[slot]
                block = grads[j, slot, c]
                upper = jnp.where(own_row, block, 0.0)
                lower = block - upper
                upper_left = jnp.where(left_col, upper, 0.0)
                lower_left = jnp.where(left_col, lower, 0.0)
                terms = (upper_left, upper - upper_left, lower_left, lower - lower_left)
                sums = [a + b for a, b in zip(sums, terms)]
            own_sum[j, c, :, :PIX] = sums[0]
            own_sum[j, c, :, PIX:] = sums[1]
            next_sum[j, c, :, :PIX] = sums[2]
            next_sum[j, c, :, PIX:] = sums[3]
        next_copy(j).start()

    def object_store(j, c):
        return pltpu.make_async_copy(own_sum.at[j, c], (new_real, new_imag)[c].at[j], store_sem.at[j, c])

    def probe_store(c):
        return pltpu.make_async_copy(new_probe.at[c], (new_probe_real, new_probe_imag)[c], store_sem.at[GROUP, c])

    def finish_slice(j):
        next_copy(j).wait_recv()
        for c in range(2):
            own_sum[j, c] = objects[c][j] - OBJ_STEP * (own_sum[j, c] + next_recv[j, c])
            object_store(j, c).start()

    core_copy.start()
    core_copy.wait_recv()
    for n in range(n_column):
        column[n] = parts[core, n] + core_recv[n]
    column_recv[column_spot] = column[column_spot]
    start_all(column_copy, n_column)
    release(1)
    gather_slice(2)

    wait_got(column_recv, column_send_sem, column_recv_sem, column_peer, n_column)
    total = column_recv[0]
    for i in range(1, n_column):
        total = total + column_recv[i]
    plane[...] = total
    plane_recv[plane_spot] = plane[depth]
    start_all(plane_copy, n_line * n_depth)
    release(0)

    gather_slice(1)

    wait_got(plane_recv, plane_send_sem, plane_recv_sem, plane_peer, n_line * n_depth)
    total = plane_recv[0]
    for i in range(1, n_line * n_depth):
        total = total + plane_recv[i]
    final[spot] = total
    start_all(final_copy, ring)

    gather_slice(0)
    finish_slice(2)
    finish_slice(1)
    wait_got(final, final_send_sem, final_recv_sem, ring_peer, ring)
    live_total = lax.fori_loop(0, n_tile, lambda i, acc: acc + count_ref[i], 0).astype(jnp.float32)
    for c, source in ((0, probe_real), (1, probe_imag)):
        for m in range(2):
            for i in range(0, quarter, 8):
                flat = (c * 2 + m) * quarter + i
                grad = final[flat // height, flat % height : flat % height + 8]
                start = pl.multiple_of(depth * quarter + i, 8)
                new_probe[c, m, i : i + 8] = source[m, pl.ds(start, 8)] - PROBE_STEP * grad / live_total
        probe_store(c).start()
    finish_slice(0)

    for j in range(GROUP):
        for c in range(2):
            head_copy(j, c).wait_send()
        each_patch_send(j, wait_send)

        next_copy(j).wait_send()

    def piece_sent(k, carry):
        @pl.when(jnp.logical_and(k // GROUP != depth, jnp.logical_or(k == 0, k >= GROUP)))
        def _():
            piece_copy(k).wait_send()

        return carry

    lax.fori_loop(0, SLICES, piece_sent, 0)
    for c in range(2):
        for j in range(GROUP):
            object_store(j, c).wait()
        probe_store(c).wait()
    core_copy.wait_send()
    wait_sent(column_copy, n_column)
    wait_sent(plane_copy, n_line * n_depth)
    wait_sent(final_copy, ring)


def hand_over(*refs):
    sources, targets, held, load_sem, store_sem = refs[:4], refs[4:8], refs[8:12], refs[12], refs[13]
    chunks = []
    for i in range(4):
        for n in range(sources[i].shape[0]):
            at = (i, n)
            chunks.append((
                pltpu.make_async_copy(sources[i].at[n], held[i].at[n], load_sem.at[at]),
                pltpu.make_async_copy(held[i].at[n], targets[i].at[n], store_sem.at[at]),
            ))
    for load, _ in chunks:
        load.start()
    for load, store in chunks:
        load.wait()
        store.start()
    for _, store in chunks:
        store.wait()


def body(
    object_real, object_imag, probe_real, probe_imag, measured, row_offset, col_offset, counts
):
    n_tile, n_depth = lax.axis_size("tile"), lax.axis_size("depth")
    ring = min(RING, n_tile // 2)
    n_line = n_tile // ring
    slab = object_real.shape
    cols = slab[2]
    height = PIX // ring
    hbm = pl.BlockSpec(memory_space=pltpu.HBM)
    smem = pltpu.SMEM
    f32 = jnp.float32
    dma = pltpu.SemaphoreType.DMA
    results = pl.pallas_call(
        functools.partial(kernel, n_tile, n_depth, ring),
        out_shape=(
            jax.ShapeDtypeStruct(slab, f32),
            jax.ShapeDtypeStruct(slab, f32),
            jax.ShapeDtypeStruct((2, PIX // n_depth, PIX), f32),
            jax.ShapeDtypeStruct((2, PIX // n_depth, PIX), f32),
        ),
        in_specs=[hbm] * 9,
        out_specs=(hbm,) * 4,
        scratch_shapes=[
            pltpu.VMEM((GROUP, 2, PIX, cols), f32),
            pltpu.VMEM((GROUP, n_depth, 2, PIX, PIX), f32),
            pltpu.VMEM((SLICES, 2, PIX, PIX), f32),
            pltpu.VMEM((SLICES + 1, 2, 2, PIX, PIX), f32),
            pltpu.VMEM((SLICES, 2, PIX, PIX), f32),
            pltpu.VMEM((GROUP, n_depth, 2, PIX, PIX), f32),
            pltpu.VMEM((GROUP, 2, PIX, cols), f32),
            pltpu.VMEM((GROUP, 2, PIX, cols), f32),
            pltpu.VMEM((GROUP, 2, PIX, cols), f32),
            pltpu.VMEM((2, ring // 2, n_depth, height, PIX), f32),
            pltpu.VMEM((ring // 2, n_depth, height, PIX), f32),
            pltpu.VMEM((ring // 2, n_depth, height, PIX), f32),
            pltpu.VMEM((ring // 2, n_depth, height, PIX), f32),
            pltpu.VMEM((n_depth, height, PIX), f32),
            pltpu.VMEM((n_line * n_depth, height, PIX), f32),
            pltpu.VMEM((ring, height, PIX), f32),
            smem(row_offset.shape, jnp.int32), smem(col_offset.shape, jnp.int32), smem(counts.shape, jnp.int32),
            pltpu.VMEM(slab, f32), pltpu.VMEM(slab, f32),
            pltpu.VMEM(probe_real.shape, f32), pltpu.VMEM(probe_real.shape, f32),
            pltpu.VMEM(measured.shape[1:], f32),
            *[pltpu.VMEM(s, jnp.bfloat16) for s in ((6 * PIX, 2 * PIX), (2 * PIX, 6 * PIX))] * 2,
            pltpu.VMEM((4, PIX, PIX), f32), dma((9,)),
            pltpu.VMEM((2, 2, PIX // n_depth, PIX), f32), dma((GROUP + 1, 2)),
            dma((GROUP, 2)), dma((GROUP, 2)), dma((GROUP, n_depth)), dma((SLICES,)),
            dma((SLICES,)), dma((GROUP, n_depth)), dma((GROUP,)), dma((GROUP,)),
            dma((2,)), dma((ring // 2,)), dma((ring // 2,)),
            dma((n_line * n_depth,)), dma((n_line * n_depth,)), dma((ring,)), dma((ring,)),
        ],
        compiler_params=pltpu.CompilerParams(
            collective_id=0, has_side_effects=True, vmem_limit_bytes=60 * 1024 * 1024
        ),
    )(
        row_offset, col_offset, counts, object_real, object_imag, probe_real, probe_imag, measured,
        jnp.asarray(make_constants()),
    )
    return pl.pallas_call(
        hand_over,
        out_shape=tuple(jax.ShapeDtypeStruct(r.shape, r.dtype) for r in results),
        in_specs=[hbm] * 4,
        out_specs=(hbm,) * 4,
        scratch_shapes=[pltpu.VMEM(r.shape, r.dtype) for r in results] + [dma((4, GROUP)), dma((4, GROUP))],
        compiler_params=pltpu.CompilerParams(vmem_limit_bytes=60 * 1024 * 1024),
    )(*results)


def solution(mesh):
    placed = (
        P("depth", "tile", None),
        P("depth", "tile", None),
        P(),
        P(),
        P("tile", None, None),
        P("tile"),
        P("tile"),
        P(),
    )
    return jax.shard_map(
        body,
        mesh=mesh,
        in_specs=placed,
        out_specs=(
            P("depth", "tile", None),
            P("depth", "tile", None),
            P(None, "depth", None),
            P(None, "depth", None),
        ),
        check_vma=False,
    )
```

```python
import functools

import jax
import jax.numpy as jnp
import numpy as np
from jax import lax
from jax.experimental import pallas as pl
from jax.experimental.pallas import tpu as pltpu
from jax.sharding import PartitionSpec as P

PIX = 128
SLICES = 12
GROUP = 3
RING = 16
PROP_PHASE = 12.0
AMP_EPS = 0.05
OBJ_STEP = 1.0
PROBE_STEP = 4.0


def make_constants():
    n = np.arange(PIX)
    dft = np.exp(-2j * np.pi * ((n[:, None] * n[None, :]) % PIX) / PIX) / np.sqrt(PIX)
    freq = ((n + PIX // 2) % PIX - PIX // 2) / PIX
    step = np.conj(dft) @ (np.exp(-1j * PROP_PHASE * freq**2)[:, None] * dft)
    return np.stack([step.real, step.imag, dft.real, dft.imag]).astype(np.float32)


def split(value):
    high = value.astype(jnp.bfloat16)
    low = (value - high.astype(jnp.float32)).astype(jnp.bfloat16)
    return high, low


def make_factors(real, imag, right, left):
    for i, line in enumerate(((real, imag), (-imag, real))):
        high, low = split(jnp.concatenate(line, axis=1))
        for n, part in enumerate((high, high, low)):
            right[2 * n * PIX + i * PIX : 2 * n * PIX + (i + 1) * PIX] = part
    for i, line in enumerate(((real, -imag), (imag, real))):
        high, low = split(jnp.concatenate(line, axis=1))
        for n, part in enumerate((high, high, low)):
            left[i * PIX : (i + 1) * PIX, 2 * n * PIX : 2 * (n + 1) * PIX] = part


def sandwich(field, right, left):
    middle = []
    for m in range(2):
        high, low = split(jnp.concatenate([field[0][m], field[1][m]], axis=1))
        wide = jnp.concatenate([high, low, high], axis=1)
        middle.append(jnp.dot(wide, right, preferred_element_type=jnp.float32))
    done = []
    for m in range(2):
        high, low = split(jnp.concatenate([middle[m][:, :PIX], middle[m][:, PIX:]], axis=0))
        tall = jnp.concatenate([high, low, high], axis=0)
        done.append(jnp.dot(left, tall, preferred_element_type=jnp.float32))
    return [[done[m][c * PIX : (c + 1) * PIX] for m in range(2)] for c in range(2)]


def times(patch_real, patch_imag, field):
    real = [field[0][m] * patch_real - field[1][m] * patch_imag for m in range(2)]
    imag = [field[0][m] * patch_imag + field[1][m] * patch_real for m in range(2)]
    return [real, imag]


MESH = pl.DeviceIdType.MESH


def turned(block, rows, cols):
    return pltpu.roll(pltpu.roll(block, rows, 0), cols, 1)


def kernel(
    n_tile, n_depth, ring,
    row_hbm, col_hbm, count_hbm, real_hbm, imag_hbm, probe_real_hbm, probe_imag_hbm, measured_hbm,
    table_hbm,
    new_real, new_imag, new_probe_real, new_probe_imag,
    head, stage, patch_ref, waves, piece_stage, grads, own_sum, next_sum, next_recv,
    parts, core_recv, column, column_recv, plane, plane_recv, final,
    row_ref, col_ref, count_ref, obj_real, obj_imag, probe_real, probe_imag, measured_ref,
    step_right, step_left, dft_right, dft_left, table, load_sem, new_probe, store_sem,
    head_send_sem, head_recv_sem, patch_send_sem, patch_recv_sem, piece_send_sem, grad_recv_sem,
    next_send_sem, next_recv_sem,
    core_sem, column_send_sem, column_recv_sem, plane_send_sem, plane_recv_sem, final_send_sem, final_recv_sem,
    last_send_sem, last_recv_sem, relay, half_send_sem, half_recv_sem, in_send_sem, in_recv_sem, out_send_sem,
):
    objects = (obj_real, obj_imag)
    sources = (real_hbm, imag_hbm)
    tile = lax.axis_index("tile")
    depth = lax.axis_index("depth")

    def fetch(n, src, dst):
        copy = pltpu.make_async_copy(src, dst, load_sem.at[n])
        copy.start()
        return copy

    offset_loads = [fetch(0, row_hbm, row_ref), fetch(1, col_hbm, col_ref)]
    object_loads = [fetch(2, real_hbm, obj_real), fetch(3, imag_hbm, obj_imag)]
    probe_loads = [fetch(4, probe_real_hbm, probe_real), fetch(5, probe_imag_hbm, probe_imag)]
    table_loads = [fetch(6, table_hbm, table)]
    far_loads = [fetch(7, measured_hbm.at[depth], measured_ref), fetch(8, count_hbm, count_ref)]

    def loaded(copies):
        for copy in copies:
            copy.wait()

    after, before = lax.rem(tile + 1, n_tile), lax.rem(tile + n_tile - 1, n_tile)
    n_line = n_tile // ring
    spot, row_of = lax.rem(tile, ring), tile // ring
    ring_base = row_of * ring

    def send(src, dst, send_sem, recv_sem, to_tile, to_depth):
        return pltpu.make_async_remote_copy(
            src_ref=src, dst_ref=dst, send_sem=send_sem, recv_sem=recv_sem,
            device_id=(to_tile, to_depth), device_id_type=MESH,
        )

    def ring_peer(i):
        return lax.rem(spot + i, ring)

    plane_spot = row_of * n_depth + depth

    def plane_peer(i):
        return lax.rem(plane_spot + i, n_line * n_depth)

    def plane_device(n):
        return (n // n_depth) * ring + spot, lax.rem(n, n_depth)

    core, column_spot, n_column = lax.rem(spot, 2), spot // 2, ring // 2

    def column_peer(i):
        return lax.rem(column_spot + i, n_column)

    def depth_peer(i):
        return lax.rem(depth + i, n_depth)

    barrier = pltpu.get_barrier_semaphore()

    def greet(to_tile, to_depth):
        pl.semaphore_signal(barrier, inc=1, device_id=(to_tile, to_depth), device_id_type=MESH)

    greet(after, depth)
    greet(before, depth)
    lax.fori_loop(1, ring, lambda i, c: (greet(ring_base + ring_peer(i), depth), c)[1], 0)
    lax.fori_loop(1, n_line * n_depth, lambda i, c: (greet(*plane_device(plane_peer(i))), c)[1], 0)
    pl.semaphore_wait(barrier, 2 + ring - 1 + n_line * n_depth - 1)

    def head_copy(j, c):
        return send(sources[c].at[j], head.at[j, c], head_send_sem.at[j, c], head_recv_sem.at[j, c], before, depth)

    def start_head(j):
        for c in range(2):
            head_copy(j, c).start()

    start_head(0)

    row_iota = lax.broadcasted_iota(jnp.int32, (PIX, PIX), 0)
    col_iota = lax.broadcasted_iota(jnp.int32, (PIX, PIX), 1)

    def patch_copy(j, to):
        k = depth * GROUP + j
        return send(
            stage.at[j, to], patch_ref.at[k], patch_send_sem.at[j, to], patch_recv_sem.at[k], tile, to
        )

    def each_patch_send(j, act):
        for i in (2, 1, 3):
            act(patch_copy(j, depth_peer(i)))

    def start(copy):
        copy.start()

    def wait_send(copy):
        copy.wait_send()

    def cut(j, i):
        slot = depth_peer(i)
        row, col = row_ref[slot], col_ref[slot]
        own_row, left_col = row_iota >= row, col_iota >= col
        out = []
        for c in range(2):
            upper = jnp.where(left_col, objects[c][j, :, :PIX], objects[c][j, :, PIX:])
            lower = jnp.where(left_col, head[j, c, :, :PIX], head[j, c, :, PIX:])
            block = jnp.where(own_row, upper, lower)
            out.append(turned(block, lax.rem(PIX - row, PIX), lax.rem(PIX - col + PIX, PIX)))
        return slot, out

    def cut_slice(j, carry):
        for c in range(2):
            head_copy(j, c).wait_recv()

        @pl.when(j + 1 < GROUP)
        def _():
            start_head(j + 1)

        def cut_slot(i, carry):
            slot, out = cut(j, i)
            for c in range(2):
                stage[j, slot, c] = out[c]
            return carry

        lax.fori_loop(1, n_depth, cut_slot, 0)

        each_patch_send(j, start)
        _, out = cut(j, 0)
        for c in range(2):
            patch_ref[depth * GROUP + j, c] = out[c]
        return carry

    loaded(offset_loads)
    loaded(object_loads)
    lax.fori_loop(0, GROUP, cut_slice, 0)

    def load(ref, k):
        return [[ref[k, c, m] for m in range(2)] for c in range(2)]

    def store(ref, k, field):
        for c in range(2):
            for m in range(2):
                ref[k, c, m] = field[c][m]

    def patch_ready(k):
        @pl.when(k // GROUP != depth)
        def _():
            send(stage.at[0, 0], patch_ref.at[k], patch_send_sem.at[0, 0], patch_recv_sem.at[k], tile, depth).wait_recv()

    loaded(probe_loads)
    loaded(table_loads)
    make_factors(table[0], table[1], step_right, step_left)
    make_factors(table[2], table[3], dft_right, dft_left)
    store(waves, 0, [[probe_real[m] for m in range(2)], [probe_imag[m] for m in range(2)]])

    def forward(k, carry):
        patch_ready(k)

        chi = times(patch_ref[k, 0], patch_ref[k, 1], load(waves, k))
        store(waves, k + 1, sandwich(chi, step_right[...], step_left[...]))
        return carry

    last = SLICES - 1
    lax.fori_loop(0, last, forward, 0)
    patch_ready(last)
    loaded(far_loads)
    exit_wave = times(patch_ref[last, 0], patch_ref[last, 1], load(waves, last))
    far = sandwich(exit_wave, dft_right[...], dft_left[...])
    intensity = sum(far[c][m] * far[c][m] for c in range(2) for m in range(2))
    live = jnp.where(depth < count_ref[tile], 1.0, 0.0)
    factor = (1.0 - measured_ref[...] * lax.rsqrt(intensity + AMP_EPS)) * live
    bent = [[far[0][m] * factor for m in range(2)], [-far[1][m] * factor for m in range(2)]]
    store(waves, SLICES, sandwich(bent, dft_right[...], dft_left[...]))

    own_turn = (row_ref[depth], col_ref[depth])

    def collect(k, grad):
        wave = load(waves, k)
        real = sum(wave[0][m] * grad[0][m] - wave[1][m] * grad[1][m] for m in range(2))
        imag = -sum(wave[0][m] * grad[1][m] + wave[1][m] * grad[0][m] for m in range(2))
        row, col = own_turn
        piece_stage[k, 0] = turned(real, row, lax.rem(col, PIX))
        piece_stage[k, 1] = turned(imag, row, lax.rem(col, PIX))
        return times(patch_ref[k, 0], patch_ref[k, 1], grad)

    def piece_copy(k):
        j = lax.rem(k, GROUP)
        return send(
            piece_stage.at[k], grads.at[j, depth], piece_send_sem.at[k], grad_recv_sem.at[j, depth], tile, k // GROUP
        )

    def last_copy(c):
        return send(
            piece_stage.at[0, c], grads.at[0, depth, c], last_send_sem.at[c], last_recv_sem.at[depth, c], tile, 0
        )

    def half_copy():
        return send(
            piece_stage.at[1, 0], grads.at[1, depth, 0], half_send_sem.at[0], half_recv_sem.at[0], tile, 0
        )

    def relay_in_copy(j):
        return send(piece_stage.at[j, 1], relay.at[j], in_send_sem.at[j], in_recv_sem.at[j], tile, 1)

    def relay_out_copy(j):
        sem = last_recv_sem.at[2, 1] if j == 0 else half_recv_sem.at[1]
        return send(relay.at[j], grads.at[j, 2, 1], out_send_sem.at[j], sem, tile, 0)

    def start_piece(k):
        @pl.when(k // GROUP != depth)
        def _():
            piece_copy(k).start()

    def start_piece_one():
        @pl.when(lax.rem(depth, 2) == 1)
        def _():
            piece_copy(1).start()

        @pl.when(depth == 2)
        def _():
            half_copy().start()
            relay_in_copy(1).start()

    def start_last(c):
        @pl.when(lax.rem(depth, 2) == 1)
        def _():
            last_copy(c).start()

    def start_last_of_two():
        @pl.when(depth == 2)
        def _():
            last_copy(0).start()
            relay_in_copy(0).start()

    def pass_on(j):
        @pl.when(depth == 1)
        def _():
            relay_in_copy(j).wait_recv()
            relay_out_copy(j).start()

    def deliver(k):
        @pl.when(k // GROUP == depth)
        def _():
            grads[lax.rem(k, GROUP), depth] = piece_stage[k]

        @pl.when(lax.rem(k, GROUP) == GROUP - 1)
        def _():
            start_piece(k)

        @pl.when(k == 4)
        def _():
            start_piece(10)

    def backward(i, carry):
        k = last - i
        bent = collect(k, load(waves, SLICES))
        store(waves, SLICES, sandwich(bent, step_right[...], step_left[...]))
        deliver(k)
        return carry

    lax.fori_loop(0, last, backward, 0)
    entry = collect(0, load(waves, SLICES))
    deliver(0)

    quarter = PIX // n_depth
    height = 4 * quarter // ring
    for c in range(2):
        for m in range(2):
            value = entry[c][m] if c == 0 else -entry[c][m]
            for d in range(n_depth):
                for i in range(0, quarter, 8):
                    flat = (c * 2 + m) * quarter + i
                    part = flat // height
                    parts[part % 2, part // 2, d, flat % height : flat % height + 8] = value[
                        d * quarter + i : d * quarter + i + 8
                    ]

    core_copy = send(parts.at[1 - core], core_recv, core_sem.at[0], core_sem.at[1], tile + 1 - 2 * core, depth)

    def column_copy(i):
        to = column_peer(i)
        return send(
            column.at[to], column_recv.at[column_spot], column_send_sem.at[to], column_recv_sem.at[column_spot],
            ring_base + 2 * to + core, depth,
        )

    def plane_copy(i):
        to = plane_peer(i)
        to_tile, to_depth = plane_device(to)
        return send(
            plane.at[to_depth], plane_recv.at[plane_spot], plane_send_sem.at[to], plane_recv_sem.at[plane_spot],
            to_tile, to_depth,
        )

    def final_copy(i):
        to = ring_peer(i)
        return send(
            final.at[spot], final.at[spot], final_send_sem.at[to], final_recv_sem.at[spot],
            ring_base + to, depth,
        )

    def start_all(copy, count):
        lax.fori_loop(1, count, lambda i, c: (copy(i).start(), c)[1], 0)

    def wait_sent(copy, count):
        lax.fori_loop(1, count, lambda i, c: (copy(i).wait_send(), c)[1], 0)

    def wait_got(buffer, send_sem, recv_sem, peer, count):
        def one(i, carry):
            frm = peer(i)
            send(buffer.at[frm], buffer.at[frm], send_sem.at[frm], recv_sem.at[frm], tile, depth).wait_recv()
            return carry

        lax.fori_loop(1, count, one, 0)

    def next_copy(j, c):
        return send(
            next_sum.at[j, c], next_recv.at[j, c], next_send_sem.at[j, c], next_recv_sem.at[j, c], after, depth
        )

    def arrived(j, i):
        frm = depth_peer(i)
        sem = grad_recv_sem.at[j, frm]
        send(grads.at[j, frm], grads.at[j, frm], sem, sem, tile, depth).wait_recv()

    def half_arrived(c, i):
        frm = depth_peer(i)
        sem = last_recv_sem.at[frm, c]
        send(grads.at[0, frm, c], grads.at[0, frm, c], sem, sem, tile, depth).wait_recv()

    def gather_half(j, c):
        sums = [0.0] * 4
        for slot in range(n_depth):
            own_row, left_col = row_iota >= row_ref[slot], col_iota >= col_ref[slot]
            block = grads[j, slot, c]
            upper = jnp.where(own_row, block, 0.0)
            lower = block - upper
            upper_left = jnp.where(left_col, upper, 0.0)
            lower_left = jnp.where(left_col, lower, 0.0)
            terms = (upper_left, upper - upper_left, lower_left, lower - lower_left)
            sums = [a + b for a, b in zip(sums, terms)]
        own_sum[j, c, :, :PIX] = sums[0]
        own_sum[j, c, :, PIX:] = sums[1]
        next_sum[j, c, :, :PIX] = sums[2]
        next_sum[j, c, :, PIX:] = sums[3]
        next_copy(j, c).start()

    def gather_slice(j):
        if j == 2:
            for i in range(1, n_depth):
                arrived(j, i)
        elif j == 1:
            arrived(j, 1)
            arrived(j, 3)

            @pl.when(depth == 0)
            def _():
                for c in range(2):
                    sem, half = half_recv_sem.at[c], grads.at[1, 2, c]
                    send(half, half, sem, sem, tile, depth).wait_recv()

            @pl.when(depth != 0)
            def _():
                arrived(j, 2)

        else:
            @pl.when(depth != 0)
            def _():
                for i in range(1, n_depth):
                    arrived(j, i)

        def half(c, carry):
            if j == 0:
                @pl.when(depth == 0)
                def _():
                    for i in range(1, n_depth):
                        half_arrived(c, i)

            gather_half(j, c)
            return carry

        lax.fori_loop(0, 2, half, 0)

    def object_store(j, c):
        return pltpu.make_async_copy(own_sum.at[j, c], (new_real, new_imag)[c].at[j], store_sem.at[j, c])

    def probe_store(c):
        return pltpu.make_async_copy(new_probe.at[c], (new_probe_real, new_probe_imag)[c], store_sem.at[GROUP, c])

    def finish_slice(j):
        for c in range(2):
            next_copy(j, c).wait_recv()
            own_sum[j, c] = objects[c][j] - OBJ_STEP * (own_sum[j, c] + next_recv[j, c])
            object_store(j, c).start()

    core_copy.start()
    start_piece(7)
    core_copy.wait_recv()
    for n in range(n_column):
        column[n] = parts[core, n] + core_recv[n]
    column_recv[column_spot] = column[column_spot]
    start_all(column_copy, n_column)
    for k in (9, 4):
        start_piece(k)
    start_piece_one()
    gather_slice(2)

    wait_got(column_recv, column_send_sem, column_recv_sem, column_peer, n_column)
    total = column_recv[0]
    for i in range(1, n_column):
        total = total + column_recv[i]
    plane[...] = total
    plane_recv[plane_spot] = plane[depth]
    start_all(plane_copy, n_line * n_depth)
    for k in (6, 3):
        start_piece(k)
    start_last(0)
    start_last_of_two()
    pass_on(1)
    gather_slice(1)

    wait_got(plane_recv, plane_send_sem, plane_recv_sem, plane_peer, n_line * n_depth)
    total = plane_recv[0]
    for i in range(1, n_line * n_depth):
        total = total + plane_recv[i]
    final[spot] = total
    start_all(final_copy, ring)
    start_last(1)
    pass_on(0)
    gather_slice(0)
    finish_slice(2)
    finish_slice(1)
    wait_got(final, final_send_sem, final_recv_sem, ring_peer, ring)
    live_total = lax.fori_loop(0, n_tile, lambda i, acc: acc + count_ref[i], 0).astype(jnp.float32)
    for c, source in ((0, probe_real), (1, probe_imag)):
        for m in range(2):
            for i in range(0, quarter, 8):
                flat = (c * 2 + m) * quarter + i
                grad = final[flat // height, flat % height : flat % height + 8]
                start = pl.multiple_of(depth * quarter + i, 8)
                new_probe[c, m, i : i + 8] = source[m, pl.ds(start, 8)] - PROBE_STEP * grad / live_total
        probe_store(c).start()
    finish_slice(0)

    for j in range(GROUP):
        for c in range(2):
            head_copy(j, c).wait_send()
        each_patch_send(j, wait_send)

        for c in range(2):
            next_copy(j, c).wait_send()

    def piece_sent(k, carry):
        @pl.when(k // GROUP != depth)
        def _():
            piece_copy(k).wait_send()

        return carry

    lax.fori_loop(2, SLICES, piece_sent, 0)

    @pl.when(lax.rem(depth, 2) == 1)
    def _():
        piece_copy(1).wait_send()
        last_copy(0).wait_send()
        last_copy(1).wait_send()

    @pl.when(depth == 2)
    def _():
        half_copy().wait_send()
        last_copy(0).wait_send()
        relay_in_copy(0).wait_send()
        relay_in_copy(1).wait_send()

    @pl.when(depth == 1)
    def _():
        relay_out_copy(0).wait_send()
        relay_out_copy(1).wait_send()

    for c in range(2):
        for j in range(GROUP):
            object_store(j, c).wait()
        probe_store(c).wait()
    core_copy.wait_send()
    wait_sent(column_copy, n_column)
    wait_sent(plane_copy, n_line * n_depth)
    wait_sent(final_copy, ring)


def hand_over(*refs):
    sources, targets, held, load_sem, store_sem = refs[:4], refs[4:8], refs[8:12], refs[12], refs[13]
    chunks = []
    for i in range(4):
        for n in range(sources[i].shape[0]):
            at = (i, n)
            chunks.append((
                pltpu.make_async_copy(sources[i].at[n], held[i].at[n], load_sem.at[at]),
                pltpu.make_async_copy(held[i].at[n], targets[i].at[n], store_sem.at[at]),
            ))
    for load, _ in chunks:
        load.start()
    for load, store in chunks:
        load.wait()
        store.start()
    for _, store in chunks:
        store.wait()


def body(
    object_real, object_imag, probe_real, probe_imag, measured, row_offset, col_offset, counts
):
    n_tile, n_depth = lax.axis_size("tile"), lax.axis_size("depth")
    ring = min(RING, n_tile // 2)
    n_line = n_tile // ring
    slab = object_real.shape
    cols = slab[2]
    height = PIX // ring
    hbm = pl.BlockSpec(memory_space=pltpu.HBM)
    smem = pltpu.SMEM
    f32 = jnp.float32
    dma = pltpu.SemaphoreType.DMA
    results = pl.pallas_call(
        functools.partial(kernel, n_tile, n_depth, ring),
        out_shape=(
            jax.ShapeDtypeStruct(slab, f32),
            jax.ShapeDtypeStruct(slab, f32),
            jax.ShapeDtypeStruct((2, PIX // n_depth, PIX), f32),
            jax.ShapeDtypeStruct((2, PIX // n_depth, PIX), f32),
        ),
        in_specs=[hbm] * 9,
        out_specs=(hbm,) * 4,
        scratch_shapes=[
            pltpu.VMEM((GROUP, 2, PIX, cols), f32),
            pltpu.VMEM((GROUP, n_depth, 2, PIX, PIX), f32),
            pltpu.VMEM((SLICES, 2, PIX, PIX), f32),
            pltpu.VMEM((SLICES + 1, 2, 2, PIX, PIX), f32),
            pltpu.VMEM((SLICES, 2, PIX, PIX), f32),
            pltpu.VMEM((GROUP, n_depth, 2, PIX, PIX), f32),
            pltpu.VMEM((GROUP, 2, PIX, cols), f32),
            pltpu.VMEM((GROUP, 2, PIX, cols), f32),
            pltpu.VMEM((GROUP, 2, PIX, cols), f32),
            pltpu.VMEM((2, ring // 2, n_depth, height, PIX), f32),
            pltpu.VMEM((ring // 2, n_depth, height, PIX), f32),
            pltpu.VMEM((ring // 2, n_depth, height, PIX), f32),
            pltpu.VMEM((ring // 2, n_depth, height, PIX), f32),
            pltpu.VMEM((n_depth, height, PIX), f32),
            pltpu.VMEM((n_line * n_depth, height, PIX), f32),
            pltpu.VMEM((ring, height, PIX), f32),
            smem(row_offset.shape, jnp.int32), smem(col_offset.shape, jnp.int32), smem(counts.shape, jnp.int32),
            pltpu.VMEM(slab, f32), pltpu.VMEM(slab, f32),
            pltpu.VMEM(probe_real.shape, f32), pltpu.VMEM(probe_real.shape, f32),
            pltpu.VMEM(measured.shape[1:], f32),
            *[pltpu.VMEM(s, jnp.bfloat16) for s in ((6 * PIX, 2 * PIX), (2 * PIX, 6 * PIX))] * 2,
            pltpu.VMEM((4, PIX, PIX), f32), dma((9,)),
            pltpu.VMEM((2, 2, PIX // n_depth, PIX), f32), dma((GROUP + 1, 2)),
            dma((GROUP, 2)), dma((GROUP, 2)), dma((GROUP, n_depth)), dma((SLICES,)),
            dma((SLICES,)), dma((GROUP, n_depth)), dma((GROUP, 2)), dma((GROUP, 2)),
            dma((2,)), dma((ring // 2,)), dma((ring // 2,)),
            dma((n_line * n_depth,)), dma((n_line * n_depth,)), dma((ring,)), dma((ring,)),
            dma((2,)), dma((n_depth, 2)), pltpu.VMEM((2, PIX, PIX), f32),
            dma((1,)), dma((2,)), dma((2,)), dma((2,)), dma((2,)),
        ],
        compiler_params=pltpu.CompilerParams(
            collective_id=0, has_side_effects=True, vmem_limit_bytes=60 * 1024 * 1024
        ),
    )(
        row_offset, col_offset, counts, object_real, object_imag, probe_real, probe_imag, measured,
        jnp.asarray(make_constants()),
    )
    return pl.pallas_call(
        hand_over,
        out_shape=tuple(jax.ShapeDtypeStruct(r.shape, r.dtype) for r in results),
        in_specs=[hbm] * 4,
        out_specs=(hbm,) * 4,
        scratch_shapes=[pltpu.VMEM(r.shape, r.dtype) for r in results] + [dma((4, GROUP)), dma((4, GROUP))],
        compiler_params=pltpu.CompilerParams(vmem_limit_bytes=60 * 1024 * 1024),
    )(*results)


def solution(mesh):
    placed = (
        P("depth", "tile", None),
        P("depth", "tile", None),
        P(),
        P(),
        P("tile", None, None),
        P("tile"),
        P("tile"),
        P(),
    )
    return jax.shard_map(
        body,
        mesh=mesh,
        in_specs=placed,
        out_specs=(
            P("depth", "tile", None),
            P("depth", "tile", None),
            P(None, "depth", None),
            P(None, "depth", None),
        ),
        check_vma=False,
    )
```

```python
import functools

import jax
import jax.numpy as jnp
import numpy as np
from jax import lax
from jax.experimental import pallas as pl
from jax.experimental.pallas import tpu as pltpu
from jax.sharding import PartitionSpec as P

PIX = 128
SLICES = 12
GROUP = 3
RING = 16
PROP_PHASE = 12.0
AMP_EPS = 0.05
OBJ_STEP = 1.0
PROBE_STEP = 4.0


def make_constants():
    n = np.arange(PIX)
    dft = np.exp(-2j * np.pi * ((n[:, None] * n[None, :]) % PIX) / PIX) / np.sqrt(PIX)
    freq = ((n + PIX // 2) % PIX - PIX // 2) / PIX
    step = np.conj(dft) @ (np.exp(-1j * PROP_PHASE * freq**2)[:, None] * dft)
    return np.stack([step.real, step.imag, dft.real, dft.imag]).astype(np.float32)


def split(value):
    high = value.astype(jnp.bfloat16)
    low = (value - high.astype(jnp.float32)).astype(jnp.bfloat16)
    return high, low


def make_factors(real, imag, right, left):
    for i, line in enumerate(((real, imag), (-imag, real))):
        high, low = split(jnp.concatenate(line, axis=1))
        for n, part in enumerate((high, high, low)):
            right[2 * n * PIX + i * PIX : 2 * n * PIX + (i + 1) * PIX] = part
    for i, line in enumerate(((real, -imag), (imag, real))):
        high, low = split(jnp.concatenate(line, axis=1))
        for n, part in enumerate((high, high, low)):
            left[i * PIX : (i + 1) * PIX, 2 * n * PIX : 2 * (n + 1) * PIX] = part


def sandwich(field, right, left):
    middle = []
    for m in range(2):
        high, low = split(jnp.concatenate([field[0][m], field[1][m]], axis=1))
        wide = jnp.concatenate([high, low, high], axis=1)
        middle.append(jnp.dot(wide, right, preferred_element_type=jnp.float32))
    done = []
    for m in range(2):
        high, low = split(jnp.concatenate([middle[m][:, :PIX], middle[m][:, PIX:]], axis=0))
        tall = jnp.concatenate([high, low, high], axis=0)
        done.append(jnp.dot(left, tall, preferred_element_type=jnp.float32))
    return [[done[m][c * PIX : (c + 1) * PIX] for m in range(2)] for c in range(2)]


def times(patch_real, patch_imag, field):
    real = [field[0][m] * patch_real - field[1][m] * patch_imag for m in range(2)]
    imag = [field[0][m] * patch_imag + field[1][m] * patch_real for m in range(2)]
    return [real, imag]


MESH = pl.DeviceIdType.MESH


def turned(block, rows, cols):
    return pltpu.roll(pltpu.roll(block, rows, 0), cols, 1)


def kernel(
    n_tile, n_depth, ring,
    row_hbm, col_hbm, count_hbm, real_hbm, imag_hbm, probe_real_hbm, probe_imag_hbm, measured_hbm,
    table_hbm,
    new_real, new_imag, new_probe_real, new_probe_imag,
    head, stage, patch_ref, waves, piece_stage, grads, own_sum, next_sum, next_recv,
    parts, core_recv, column, column_recv, plane, plane_recv, final,
    row_ref, col_ref, count_ref, obj_real, obj_imag, probe_real, probe_imag, measured_ref,
    step_right, step_left, dft_right, dft_left, table, load_sem, new_probe, store_sem,
    head_send_sem, head_recv_sem, patch_send_sem, patch_recv_sem, piece_send_sem, grad_recv_sem,
    next_send_sem, next_recv_sem,
    core_sem, column_send_sem, column_recv_sem, plane_send_sem, plane_recv_sem, final_send_sem, final_recv_sem,
    last_send_sem, last_recv_sem, relay, half_send_sem, half_recv_sem, in_send_sem, in_recv_sem, out_send_sem,
):
    objects = (obj_real, obj_imag)
    sources = (real_hbm, imag_hbm)
    tile = lax.axis_index("tile")
    depth = lax.axis_index("depth")

    after, before = lax.rem(tile + 1, n_tile), lax.rem(tile + n_tile - 1, n_tile)
    n_line = n_tile // ring
    spot, row_of = lax.rem(tile, ring), tile // ring
    ring_base = row_of * ring

    def send(src, dst, send_sem, recv_sem, to_tile, to_depth):
        return pltpu.make_async_remote_copy(
            src_ref=src, dst_ref=dst, send_sem=send_sem, recv_sem=recv_sem,
            device_id=(to_tile, to_depth), device_id_type=MESH,
        )

    def ring_peer(i):
        return lax.rem(spot + i, ring)

    plane_spot = row_of * n_depth + depth

    def plane_peer(i):
        return lax.rem(plane_spot + i, n_line * n_depth)

    def plane_device(n):
        return (n // n_depth) * ring + spot, lax.rem(n, n_depth)

    core, column_spot, n_column = lax.rem(spot, 2), spot // 2, ring // 2

    def column_peer(i):
        return lax.rem(column_spot + i, n_column)

    def depth_peer(i):
        return lax.rem(depth + i, n_depth)

    barrier = pltpu.get_barrier_semaphore()

    def greet(to_tile, to_depth):
        pl.semaphore_signal(barrier, inc=1, device_id=(to_tile, to_depth), device_id_type=MESH)

    greet(after, depth)
    greet(before, depth)
    lax.fori_loop(1, ring, lambda i, c: (greet(ring_base + ring_peer(i), depth), c)[1], 0)
    lax.fori_loop(1, n_line * n_depth, lambda i, c: (greet(*plane_device(plane_peer(i))), c)[1], 0)
    def fetch(n, src, dst):
        copy = pltpu.make_async_copy(src, dst, load_sem.at[n])
        copy.start()
        return copy

    offset_loads = [fetch(0, row_hbm, row_ref), fetch(1, col_hbm, col_ref)]
    object_loads = [fetch(2, real_hbm, obj_real), fetch(3, imag_hbm, obj_imag)]
    probe_loads = [fetch(4, probe_real_hbm, probe_real), fetch(5, probe_imag_hbm, probe_imag)]
    table_loads = [fetch(6, table_hbm, table)]
    far_loads = [fetch(7, measured_hbm.at[depth], measured_ref), fetch(8, count_hbm, count_ref)]

    def loaded(copies):
        for copy in copies:
            copy.wait()

    pl.semaphore_wait(barrier, 2 + ring - 1 + n_line * n_depth - 1)

    def head_copy(j, c):
        return send(sources[c].at[j], head.at[j, c], head_send_sem.at[j, c], head_recv_sem.at[j, c], before, depth)

    def start_head(j):
        for c in range(2):
            head_copy(j, c).start()

    start_head(0)

    row_iota = lax.broadcasted_iota(jnp.int32, (PIX, PIX), 0)
    col_iota = lax.broadcasted_iota(jnp.int32, (PIX, PIX), 1)

    def patch_copy(j, c, to):
        k = depth * GROUP + j
        return send(
            stage.at[j, to, c], patch_ref.at[k, c], patch_send_sem.at[j, to, c], patch_recv_sem.at[k, c], tile, to
        )

    def cut(j, c, i):
        slot = depth_peer(i)
        row, col = row_ref[slot], col_ref[slot]
        own_row, left_col = row_iota >= row, col_iota >= col
        upper = jnp.where(left_col, objects[c][j, :, :PIX], objects[c][j, :, PIX:])
        lower = jnp.where(left_col, head[j, c, :, :PIX], head[j, c, :, PIX:])
        block = jnp.where(own_row, upper, lower)
        return turned(block, lax.rem(PIX - row, PIX), lax.rem(PIX - col + PIX, PIX))

    def cut_slice(j, carry):
        for c in range(2):
            head_copy(j, c).wait_recv()
            if c == 1:
                @pl.when(j + 1 < GROUP)
                def _():
                    start_head(j + 1)

            for i in (2, 1, 3):
                slot = depth_peer(i)
                stage[j, slot, c] = cut(j, c, i)
                patch_copy(j, c, slot).start()
            patch_ref[depth * GROUP + j, c] = cut(j, c, 0)
        return carry

    loaded(offset_loads)
    loaded(object_loads)
    lax.fori_loop(0, GROUP, cut_slice, 0)

    def load(ref, k):
        return [[ref[k, c, m] for m in range(2)] for c in range(2)]

    def store(ref, k, field):
        for c in range(2):
            for m in range(2):
                ref[k, c, m] = field[c][m]

    def patch_ready(k):
        @pl.when(k // GROUP != depth)
        def _():
            for c in range(2):
                sem = patch_recv_sem.at[k, c]
                send(stage.at[0, 0, 0], patch_ref.at[k, c], sem, sem, tile, depth).wait_recv()

    loaded(probe_loads)
    loaded(table_loads)
    make_factors(table[0], table[1], step_right, step_left)
    make_factors(table[2], table[3], dft_right, dft_left)
    store(waves, 0, [[probe_real[m] for m in range(2)], [probe_imag[m] for m in range(2)]])

    def forward(k, carry):
        patch_ready(k)

        chi = times(patch_ref[k, 0], patch_ref[k, 1], load(waves, k))
        store(waves, k + 1, sandwich(chi, step_right[...], step_left[...]))
        return carry

    last = SLICES - 1
    lax.fori_loop(0, last, forward, 0)
    patch_ready(last)
    loaded(far_loads)
    exit_wave = times(patch_ref[last, 0], patch_ref[last, 1], load(waves, last))
    far = sandwich(exit_wave, dft_right[...], dft_left[...])
    intensity = sum(far[c][m] * far[c][m] for c in range(2) for m in range(2))
    live = jnp.where(depth < count_ref[tile], 1.0, 0.0)
    factor = (1.0 - measured_ref[...] * lax.rsqrt(intensity + AMP_EPS)) * live
    bent = [[far[0][m] * factor for m in range(2)], [-far[1][m] * factor for m in range(2)]]
    store(waves, SLICES, sandwich(bent, dft_right[...], dft_left[...]))

    own_turn = (row_ref[depth], col_ref[depth])

    def collect(k, grad):
        wave = load(waves, k)
        real = sum(wave[0][m] * grad[0][m] - wave[1][m] * grad[1][m] for m in range(2))
        imag = -sum(wave[0][m] * grad[1][m] + wave[1][m] * grad[0][m] for m in range(2))
        row, col = own_turn
        piece_stage[k, 0] = turned(real, row, lax.rem(col, PIX))
        piece_stage[k, 1] = turned(imag, row, lax.rem(col, PIX))
        return times(patch_ref[k, 0], patch_ref[k, 1], grad)

    def piece_copy(k):
        j = lax.rem(k, GROUP)
        return send(
            piece_stage.at[k], grads.at[j, depth], piece_send_sem.at[k], grad_recv_sem.at[j, depth], tile, k // GROUP
        )

    def last_copy(c):
        return send(
            piece_stage.at[0, c], grads.at[0, depth, c], last_send_sem.at[c], last_recv_sem.at[depth, c], tile, 0
        )

    def half_copy():
        return send(
            piece_stage.at[1, 0], grads.at[1, depth, 0], half_send_sem.at[0], half_recv_sem.at[0], tile, 0
        )

    def relay_in_copy(j):
        return send(piece_stage.at[j, 1], relay.at[j], in_send_sem.at[j], in_recv_sem.at[j], tile, 1)

    def relay_out_copy(j):
        sem = last_recv_sem.at[2, 1] if j == 0 else half_recv_sem.at[1]
        return send(relay.at[j], grads.at[j, 2, 1], out_send_sem.at[j], sem, tile, 0)

    def start_piece(k):
        @pl.when(k // GROUP != depth)
        def _():
            piece_copy(k).start()

    def start_piece_one():
        @pl.when(lax.rem(depth, 2) == 1)
        def _():
            piece_copy(1).start()

        @pl.when(depth == 2)
        def _():
            half_copy().start()
            relay_in_copy(1).start()

    def start_last(c):
        @pl.when(lax.rem(depth, 2) == 1)
        def _():
            last_copy(c).start()

    def start_last_of_two():
        @pl.when(depth == 2)
        def _():
            last_copy(0).start()
            relay_in_copy(0).start()

    def pass_on(j):
        @pl.when(depth == 1)
        def _():
            relay_in_copy(j).wait_recv()
            relay_out_copy(j).start()

    def deliver(k):
        @pl.when(k // GROUP == depth)
        def _():
            grads[lax.rem(k, GROUP), depth] = piece_stage[k]

        @pl.when(lax.rem(k, GROUP) == GROUP - 1)
        def _():
            start_piece(k)

        @pl.when(k == 4)
        def _():
            start_piece(10)

    def backward(i, carry):
        k = last - i
        bent = collect(k, load(waves, SLICES))
        store(waves, SLICES, sandwich(bent, step_right[...], step_left[...]))
        deliver(k)
        return carry

    lax.fori_loop(0, last, backward, 0)
    entry = collect(0, load(waves, SLICES))
    deliver(0)

    quarter = PIX // n_depth
    height = 4 * quarter // ring
    for c in range(2):
        for m in range(2):
            value = entry[c][m] if c == 0 else -entry[c][m]
            for d in range(n_depth):
                for i in range(0, quarter, 8):
                    flat = (c * 2 + m) * quarter + i
                    part = flat // height
                    parts[part % 2, part // 2, d, flat % height : flat % height + 8] = value[
                        d * quarter + i : d * quarter + i + 8
                    ]

    core_copy = send(parts.at[1 - core], core_recv, core_sem.at[0], core_sem.at[1], tile + 1 - 2 * core, depth)

    def column_copy(i):
        to = column_peer(i)
        return send(
            column.at[to], column_recv.at[column_spot], column_send_sem.at[to], column_recv_sem.at[column_spot],
            ring_base + 2 * to + core, depth,
        )

    def plane_copy(i):
        to = plane_peer(i)
        to_tile, to_depth = plane_device(to)
        return send(
            plane.at[to_depth], plane_recv.at[plane_spot], plane_send_sem.at[to], plane_recv_sem.at[plane_spot],
            to_tile, to_depth,
        )

    def final_copy(i):
        to = ring_peer(i)
        return send(
            final.at[spot], final.at[spot], final_send_sem.at[to], final_recv_sem.at[spot],
            ring_base + to, depth,
        )

    def start_all(copy, count):
        lax.fori_loop(1, count, lambda i, c: (copy(i).start(), c)[1], 0)

    def wait_sent(copy, count):
        lax.fori_loop(1, count, lambda i, c: (copy(i).wait_send(), c)[1], 0)

    def wait_got(buffer, send_sem, recv_sem, peer, count):
        def one(i, carry):
            frm = peer(i)
            send(buffer.at[frm], buffer.at[frm], send_sem.at[frm], recv_sem.at[frm], tile, depth).wait_recv()
            return carry

        lax.fori_loop(1, count, one, 0)

    def next_copy(j, c):
        return send(
            next_sum.at[j, c], next_recv.at[j, c], next_send_sem.at[j, c], next_recv_sem.at[j, c], after, depth
        )

    def arrived(j, i):
        frm = depth_peer(i)
        sem = grad_recv_sem.at[j, frm]
        send(grads.at[j, frm], grads.at[j, frm], sem, sem, tile, depth).wait_recv()

    def half_arrived(c, i):
        frm = depth_peer(i)
        sem = last_recv_sem.at[frm, c]
        send(grads.at[0, frm, c], grads.at[0, frm, c], sem, sem, tile, depth).wait_recv()

    def gather_half(j, c):
        sums = [0.0] * 4
        for slot in range(n_depth):
            own_row, left_col = row_iota >= row_ref[slot], col_iota >= col_ref[slot]
            block = grads[j, slot, c]
            upper = jnp.where(own_row, block, 0.0)
            lower = block - upper
            upper_left = jnp.where(left_col, upper, 0.0)
            lower_left = jnp.where(left_col, lower, 0.0)
            terms = (upper_left, upper - upper_left, lower_left, lower - lower_left)
            sums = [a + b for a, b in zip(sums, terms)]
        own_sum[j, c, :, :PIX] = sums[0]
        own_sum[j, c, :, PIX:] = sums[1]
        next_sum[j, c, :, :PIX] = sums[2]
        next_sum[j, c, :, PIX:] = sums[3]
        next_copy(j, c).start()

    def gather_slice(j):
        if j == 2:
            for i in range(1, n_depth):
                arrived(j, i)
        elif j == 1:
            arrived(j, 1)
            arrived(j, 3)

            @pl.when(depth == 0)
            def _():
                for c in range(2):
                    sem, half = half_recv_sem.at[c], grads.at[1, 2, c]
                    send(half, half, sem, sem, tile, depth).wait_recv()

            @pl.when(depth != 0)
            def _():
                arrived(j, 2)

        else:
            @pl.when(depth != 0)
            def _():
                for i in range(1, n_depth):
                    arrived(j, i)

        def half(c, carry):
            if j == 0:
                @pl.when(depth == 0)
                def _():
                    for i in range(1, n_depth):
                        half_arrived(c, i)

            gather_half(j, c)
            return carry

        lax.fori_loop(0, 2, half, 0)

    def object_store(j, c):
        return pltpu.make_async_copy(own_sum.at[j, c], (new_real, new_imag)[c].at[j], store_sem.at[j, c])

    def probe_store(c):
        return pltpu.make_async_copy(new_probe.at[c], (new_probe_real, new_probe_imag)[c], store_sem.at[GROUP, c])

    def finish_slice(j):
        for c in range(2):
            next_copy(j, c).wait_recv()
            own_sum[j, c] = objects[c][j] - OBJ_STEP * (own_sum[j, c] + next_recv[j, c])
            object_store(j, c).start()

    core_copy.start()
    start_piece_one()
    core_copy.wait_recv()
    for n in range(n_column):
        column[n] = parts[core, n] + core_recv[n]
    column_recv[column_spot] = column[column_spot]
    start_all(column_copy, n_column)
    for k in (4, 7, 9):
        start_piece(k)
    gather_slice(2)

    wait_got(column_recv, column_send_sem, column_recv_sem, column_peer, n_column)
    total = column_recv[0]
    for i in range(1, n_column):
        total = total + column_recv[i]
    plane[...] = total
    plane_recv[plane_spot] = plane[depth]
    start_all(plane_copy, n_line * n_depth)
    start_last(0)
    start_last_of_two()
    pass_on(1)
    for k in (3, 6):
        start_piece(k)
    gather_slice(1)

    wait_got(plane_recv, plane_send_sem, plane_recv_sem, plane_peer, n_line * n_depth)
    total = plane_recv[0]
    for i in range(1, n_line * n_depth):
        total = total + plane_recv[i]
    final[spot] = total
    start_all(final_copy, ring)
    start_last(1)
    pass_on(0)
    gather_slice(0)
    finish_slice(2)
    finish_slice(1)
    wait_got(final, final_send_sem, final_recv_sem, ring_peer, ring)
    live_total = lax.fori_loop(0, n_tile, lambda i, acc: acc + count_ref[i], 0).astype(jnp.float32)
    for c, source in ((0, probe_real), (1, probe_imag)):
        for m in range(2):
            for i in range(0, quarter, 8):
                flat = (c * 2 + m) * quarter + i
                grad = final[flat // height, flat % height : flat % height + 8]
                start = pl.multiple_of(depth * quarter + i, 8)
                new_probe[c, m, i : i + 8] = source[m, pl.ds(start, 8)] - PROBE_STEP * grad / live_total
        probe_store(c).start()
    finish_slice(0)

    for j in range(GROUP):
        for c in range(2):
            head_copy(j, c).wait_send()
        for i in range(1, n_depth):
            for c in range(2):
                patch_copy(j, c, depth_peer(i)).wait_send()

        for c in range(2):
            next_copy(j, c).wait_send()

    def piece_sent(k, carry):
        @pl.when(k // GROUP != depth)
        def _():
            piece_copy(k).wait_send()

        return carry

    lax.fori_loop(2, SLICES, piece_sent, 0)

    @pl.when(lax.rem(depth, 2) == 1)
    def _():
        piece_copy(1).wait_send()
        last_copy(0).wait_send()
        last_copy(1).wait_send()

    @pl.when(depth == 2)
    def _():
        half_copy().wait_send()
        last_copy(0).wait_send()
        relay_in_copy(0).wait_send()
        relay_in_copy(1).wait_send()

    @pl.when(depth == 1)
    def _():
        relay_out_copy(0).wait_send()
        relay_out_copy(1).wait_send()

    for c in range(2):
        for j in range(GROUP):
            object_store(j, c).wait()
        probe_store(c).wait()
    core_copy.wait_send()
    wait_sent(column_copy, n_column)
    wait_sent(plane_copy, n_line * n_depth)
    wait_sent(final_copy, ring)


def hand_over(*refs):
    sources, targets, held, load_sem, store_sem = refs[:4], refs[4:8], refs[8:12], refs[12], refs[13]
    chunks = []
    for i in range(4):
        for n in range(sources[i].shape[0]):
            at = (i, n)
            chunks.append((
                pltpu.make_async_copy(sources[i].at[n], held[i].at[n], load_sem.at[at]),
                pltpu.make_async_copy(held[i].at[n], targets[i].at[n], store_sem.at[at]),
            ))
    for load, _ in chunks:
        load.start()
    for load, store in chunks:
        load.wait()
        store.start()
    for _, store in chunks:
        store.wait()


def body(
    object_real, object_imag, probe_real, probe_imag, measured, row_offset, col_offset, counts
):
    n_tile, n_depth = lax.axis_size("tile"), lax.axis_size("depth")
    ring = min(RING, n_tile // 2)
    n_line = n_tile // ring
    slab = object_real.shape
    cols = slab[2]
    height = PIX // ring
    hbm = pl.BlockSpec(memory_space=pltpu.HBM)
    smem = pltpu.SMEM
    f32 = jnp.float32
    dma = pltpu.SemaphoreType.DMA
    results = pl.pallas_call(
        functools.partial(kernel, n_tile, n_depth, ring),
        out_shape=(
            jax.ShapeDtypeStruct(slab, f32),
            jax.ShapeDtypeStruct(slab, f32),
            jax.ShapeDtypeStruct((2, PIX // n_depth, PIX), f32),
            jax.ShapeDtypeStruct((2, PIX // n_depth, PIX), f32),
        ),
        in_specs=[hbm] * 9,
        out_specs=(hbm,) * 4,
        scratch_shapes=[
            pltpu.VMEM((GROUP, 2, PIX, cols), f32),
            pltpu.VMEM((GROUP, n_depth, 2, PIX, PIX), f32),
            pltpu.VMEM((SLICES, 2, PIX, PIX), f32),
            pltpu.VMEM((SLICES + 1, 2, 2, PIX, PIX), f32),
            pltpu.VMEM((SLICES, 2, PIX, PIX), f32),
            pltpu.VMEM((GROUP, n_depth, 2, PIX, PIX), f32),
            pltpu.VMEM((GROUP, 2, PIX, cols), f32),
            pltpu.VMEM((GROUP, 2, PIX, cols), f32),
            pltpu.VMEM((GROUP, 2, PIX, cols), f32),
            pltpu.VMEM((2, ring // 2, n_depth, height, PIX), f32),
            pltpu.VMEM((ring // 2, n_depth, height, PIX), f32),
            pltpu.VMEM((ring // 2, n_depth, height, PIX), f32),
            pltpu.VMEM((ring // 2, n_depth, height, PIX), f32),
            pltpu.VMEM((n_depth, height, PIX), f32),
            pltpu.VMEM((n_line * n_depth, height, PIX), f32),
            pltpu.VMEM((ring, height, PIX), f32),
            smem(row_offset.shape, jnp.int32), smem(col_offset.shape, jnp.int32), smem(counts.shape, jnp.int32),
            pltpu.VMEM(slab, f32), pltpu.VMEM(slab, f32),
            pltpu.VMEM(probe_real.shape, f32), pltpu.VMEM(probe_real.shape, f32),
            pltpu.VMEM(measured.shape[1:], f32),
            *[pltpu.VMEM(s, jnp.bfloat16) for s in ((6 * PIX, 2 * PIX), (2 * PIX, 6 * PIX))] * 2,
            pltpu.VMEM((4, PIX, PIX), f32), dma((9,)),
            pltpu.VMEM((2, 2, PIX // n_depth, PIX), f32), dma((GROUP + 1, 2)),
            dma((GROUP, 2)), dma((GROUP, 2)), dma((GROUP, n_depth, 2)), dma((SLICES, 2)),
            dma((SLICES,)), dma((GROUP, n_depth)), dma((GROUP, 2)), dma((GROUP, 2)),
            dma((2,)), dma((ring // 2,)), dma((ring // 2,)),
            dma((n_line * n_depth,)), dma((n_line * n_depth,)), dma((ring,)), dma((ring,)),
            dma((2,)), dma((n_depth, 2)), pltpu.VMEM((2, PIX, PIX), f32),
            dma((1,)), dma((2,)), dma((2,)), dma((2,)), dma((2,)),
        ],
        compiler_params=pltpu.CompilerParams(
            collective_id=0, has_side_effects=True, vmem_limit_bytes=60 * 1024 * 1024
        ),
    )(
        row_offset, col_offset, counts, object_real, object_imag, probe_real, probe_imag, measured,
        jnp.asarray(make_constants()),
    )
    return pl.pallas_call(
        hand_over,
        out_shape=tuple(jax.ShapeDtypeStruct(r.shape, r.dtype) for r in results),
        in_specs=[hbm] * 4,
        out_specs=(hbm,) * 4,
        scratch_shapes=[pltpu.VMEM(r.shape, r.dtype) for r in results] + [dma((4, GROUP)), dma((4, GROUP))],
        compiler_params=pltpu.CompilerParams(vmem_limit_bytes=60 * 1024 * 1024),
    )(*results)


def solution(mesh):
    placed = (
        P("depth", "tile", None),
        P("depth", "tile", None),
        P(),
        P(),
        P("tile", None, None),
        P("tile"),
        P("tile"),
        P(),
    )
    return jax.shard_map(
        body,
        mesh=mesh,
        in_specs=placed,
        out_specs=(
            P("depth", "tile", None),
            P("depth", "tile", None),
            P(None, "depth", None),
            P(None, "depth", None),
        ),
        check_vma=False,
    )
```

```python
import functools

import jax
import jax.numpy as jnp
import numpy as np
from jax import lax
from jax.experimental import pallas as pl
from jax.experimental.pallas import tpu as pltpu
from jax.sharding import PartitionSpec as P

PIX = 128
SLICES = 12
GROUP = 3
RING = 16
PROP_PHASE = 12.0
AMP_EPS = 0.05
OBJ_STEP = 1.0
PROBE_STEP = 4.0


def make_constants():
    n = np.arange(PIX)
    dft = np.exp(-2j * np.pi * ((n[:, None] * n[None, :]) % PIX) / PIX) / np.sqrt(PIX)
    freq = ((n + PIX // 2) % PIX - PIX // 2) / PIX
    step = np.conj(dft) @ (np.exp(-1j * PROP_PHASE * freq**2)[:, None] * dft)
    return np.stack([step.real, step.imag, dft.real, dft.imag]).astype(np.float32)


def split(value):
    high = value.astype(jnp.bfloat16)
    low = (value - high.astype(jnp.float32)).astype(jnp.bfloat16)
    return high, low


def make_factors(real, imag, right, left):
    for i, line in enumerate(((real, imag), (-imag, real))):
        high, low = split(jnp.concatenate(line, axis=1))
        for n, part in enumerate((high, high, low)):
            right[2 * n * PIX + i * PIX : 2 * n * PIX + (i + 1) * PIX] = part
    for i, line in enumerate(((real, -imag), (imag, real))):
        high, low = split(jnp.concatenate(line, axis=1))
        for n, part in enumerate((high, high, low)):
            left[i * PIX : (i + 1) * PIX, 2 * n * PIX : 2 * (n + 1) * PIX] = part


def sandwich(field, right, left):
    middle = []
    for m in range(2):
        high, low = split(jnp.concatenate([field[0][m], field[1][m]], axis=1))
        wide = jnp.concatenate([high, low, high], axis=1)
        middle.append(jnp.dot(wide, right, preferred_element_type=jnp.float32))
    done = []
    for m in range(2):
        high, low = split(jnp.concatenate([middle[m][:, :PIX], middle[m][:, PIX:]], axis=0))
        tall = jnp.concatenate([high, low, high], axis=0)
        done.append(jnp.dot(left, tall, preferred_element_type=jnp.float32))
    return [[done[m][c * PIX : (c + 1) * PIX] for m in range(2)] for c in range(2)]


def times(patch_real, patch_imag, field):
    real = [field[0][m] * patch_real - field[1][m] * patch_imag for m in range(2)]
    imag = [field[0][m] * patch_imag + field[1][m] * patch_real for m in range(2)]
    return [real, imag]


MESH = pl.DeviceIdType.MESH


def turned(block, rows, cols):
    return pltpu.roll(pltpu.roll(block, rows, 0), cols, 1)


def kernel(
    n_tile, n_depth, ring,
    row_hbm, col_hbm, count_hbm, real_hbm, imag_hbm, probe_real_hbm, probe_imag_hbm, measured_hbm,
    table_hbm,
    new_real, new_imag, new_probe_real, new_probe_imag,
    head, stage, patch_ref, waves, piece_stage, grads, own_sum, next_sum, next_recv,
    parts, core_recv, column, column_recv, plane, plane_recv, final,
    row_ref, col_ref, count_ref, obj_real, obj_imag, probe_real, probe_imag, measured_ref,
    step_right, step_left, dft_right, dft_left, table, load_sem, new_probe, store_sem,
    head_send_sem, head_recv_sem, patch_send_sem, patch_recv_sem, piece_send_sem, grad_recv_sem,
    next_send_sem, next_recv_sem,
    core_sem, column_send_sem, column_recv_sem, plane_send_sem, plane_recv_sem, final_send_sem, final_recv_sem,
    last_send_sem, last_recv_sem, relay, half_send_sem, half_recv_sem, in_send_sem, in_recv_sem, out_send_sem,
):
    objects = (obj_real, obj_imag)
    sources = (real_hbm, imag_hbm)
    tile = lax.axis_index("tile")
    depth = lax.axis_index("depth")

    after, before = lax.rem(tile + 1, n_tile), lax.rem(tile + n_tile - 1, n_tile)
    n_line = n_tile // ring
    spot, row_of = lax.rem(tile, ring), tile // ring
    ring_base = row_of * ring

    def send(src, dst, send_sem, recv_sem, to_tile, to_depth):
        return pltpu.make_async_remote_copy(
            src_ref=src, dst_ref=dst, send_sem=send_sem, recv_sem=recv_sem,
            device_id=(to_tile, to_depth), device_id_type=MESH,
        )

    def ring_peer(i):
        return lax.rem(spot + i, ring)

    plane_spot = row_of * n_depth + depth

    def plane_peer(i):
        return lax.rem(plane_spot + i, n_line * n_depth)

    def plane_device(n):
        return (n // n_depth) * ring + spot, lax.rem(n, n_depth)

    core, column_spot, n_column = lax.rem(spot, 2), spot // 2, ring // 2

    def column_peer(i):
        return lax.rem(column_spot + i, n_column)

    def depth_peer(i):
        return lax.rem(depth + i, n_depth)

    barrier = pltpu.get_barrier_semaphore()

    def greet(to_tile, to_depth):
        pl.semaphore_signal(barrier, inc=1, device_id=(to_tile, to_depth), device_id_type=MESH)

    greet(after, depth)
    greet(before, depth)
    lax.fori_loop(1, ring, lambda i, c: (greet(ring_base + ring_peer(i), depth), c)[1], 0)
    lax.fori_loop(1, n_line * n_depth, lambda i, c: (greet(*plane_device(plane_peer(i))), c)[1], 0)
    def fetch(n, src, dst):
        copy = pltpu.make_async_copy(src, dst, load_sem.at[n])
        copy.start()
        return copy

    offset_loads = [fetch(0, row_hbm, row_ref), fetch(1, col_hbm, col_ref)]
    object_loads = [fetch(2, real_hbm, obj_real), fetch(3, imag_hbm, obj_imag)]
    probe_loads = [fetch(4, probe_real_hbm, probe_real), fetch(5, probe_imag_hbm, probe_imag)]
    table_loads = [fetch(6, table_hbm, table)]
    far_loads = [fetch(7, measured_hbm.at[depth], measured_ref), fetch(8, count_hbm, count_ref)]

    def loaded(copies):
        for copy in copies:
            copy.wait()

    pl.semaphore_wait(barrier, 2 + ring - 1 + n_line * n_depth - 1)

    def head_copy(j, c):
        return send(sources[c].at[j], head.at[j, c], head_send_sem.at[j, c], head_recv_sem.at[j, c], before, depth)

    def start_head(j):
        for c in range(2):
            head_copy(j, c).start()

    start_head(0)

    row_iota = lax.broadcasted_iota(jnp.int32, (PIX, PIX), 0)
    col_iota = lax.broadcasted_iota(jnp.int32, (PIX, PIX), 1)

    def patch_copy(j, c, to):
        k = depth * GROUP + j
        return send(
            stage.at[j, to, c], patch_ref.at[k, c], patch_send_sem.at[j, to, c], patch_recv_sem.at[k, c], tile, to
        )

    def cut(j, c, i):
        slot = depth_peer(i)
        row, col = row_ref[slot], col_ref[slot]
        own_row, left_col = row_iota >= row, col_iota >= col
        upper = jnp.where(left_col, objects[c][j, :, :PIX], objects[c][j, :, PIX:])
        lower = jnp.where(left_col, head[j, c, :, :PIX], head[j, c, :, PIX:])
        block = jnp.where(own_row, upper, lower)
        return turned(block, lax.rem(PIX - row, PIX), lax.rem(PIX - col + PIX, PIX))

    def cut_slice(j, carry):
        for c in range(2):
            head_copy(j, c).wait_recv()
            if c == 1:
                @pl.when(j + 1 < GROUP)
                def _():
                    start_head(j + 1)

            for i in (2, 1, 3):
                slot = depth_peer(i)
                stage[j, slot, c] = cut(j, c, i)
                patch_copy(j, c, slot).start()
            patch_ref[depth * GROUP + j, c] = cut(j, c, 0)
        return carry

    loaded(offset_loads)
    loaded(object_loads)
    lax.fori_loop(0, GROUP, cut_slice, 0)

    def load(ref, k):
        return [[ref[k, c, m] for m in range(2)] for c in range(2)]

    def store(ref, k, field):
        for c in range(2):
            for m in range(2):
                ref[k, c, m] = field[c][m]

    def patch_ready(k):
        @pl.when(k // GROUP != depth)
        def _():
            for c in range(2):
                sem = patch_recv_sem.at[k, c]
                send(stage.at[0, 0, 0], patch_ref.at[k, c], sem, sem, tile, depth).wait_recv()

    loaded(probe_loads)
    loaded(table_loads)
    make_factors(table[0], table[1], step_right, step_left)
    make_factors(table[2], table[3], dft_right, dft_left)
    store(waves, 0, [[probe_real[m] for m in range(2)], [probe_imag[m] for m in range(2)]])

    def forward(k, carry):
        patch_ready(k)

        chi = times(patch_ref[k, 0], patch_ref[k, 1], load(waves, k))
        store(waves, k + 1, sandwich(chi, step_right[...], step_left[...]))
        return carry

    last = SLICES - 1
    lax.fori_loop(0, last, forward, 0)
    patch_ready(last)
    loaded(far_loads)
    exit_wave = times(patch_ref[last, 0], patch_ref[last, 1], load(waves, last))
    far = sandwich(exit_wave, dft_right[...], dft_left[...])
    intensity = sum(far[c][m] * far[c][m] for c in range(2) for m in range(2))
    live = jnp.where(depth < count_ref[tile], 1.0, 0.0)
    factor = (1.0 - measured_ref[...] * lax.rsqrt(intensity + AMP_EPS)) * live
    bent = [[far[0][m] * factor for m in range(2)], [-far[1][m] * factor for m in range(2)]]
    store(waves, SLICES, sandwich(bent, dft_right[...], dft_left[...]))

    own_turn = (row_ref[depth], col_ref[depth])

    def collect(k, grad):
        wave = load(waves, k)
        real = sum(wave[0][m] * grad[0][m] - wave[1][m] * grad[1][m] for m in range(2))
        imag = -sum(wave[0][m] * grad[1][m] + wave[1][m] * grad[0][m] for m in range(2))
        row, col = own_turn
        piece_stage[k, 0] = turned(real, row, lax.rem(col, PIX))
        piece_stage[k, 1] = turned(imag, row, lax.rem(col, PIX))
        return times(patch_ref[k, 0], patch_ref[k, 1], grad)

    def piece_copy(k):
        j = lax.rem(k, GROUP)
        return send(
            piece_stage.at[k], grads.at[j, depth], piece_send_sem.at[k], grad_recv_sem.at[j, depth], tile, k // GROUP
        )

    def last_copy(c):
        return send(
            piece_stage.at[0, c], grads.at[0, depth, c], last_send_sem.at[c], last_recv_sem.at[depth, c], tile, 0
        )

    def half_copy():
        return send(
            piece_stage.at[1, 0], grads.at[1, depth, 0], half_send_sem.at[0], half_recv_sem.at[0], tile, 0
        )

    def relay_in_copy(j):
        return send(piece_stage.at[j, 1], relay.at[j], in_send_sem.at[j], in_recv_sem.at[j], tile, 1)

    def relay_out_copy(j):
        sem = last_recv_sem.at[2, 1] if j == 0 else half_recv_sem.at[1]
        return send(relay.at[j], grads.at[j, 2, 1], out_send_sem.at[j], sem, tile, 0)

    def start_piece(k):
        @pl.when(k // GROUP != depth)
        def _():
            piece_copy(k).start()

    def start_piece_one():
        @pl.when(lax.rem(depth, 2) == 1)
        def _():
            piece_copy(1).start()

        @pl.when(depth == 2)
        def _():
            half_copy().start()
            relay_in_copy(1).start()

    def start_last(c):
        @pl.when(lax.rem(depth, 2) == 1)
        def _():
            last_copy(c).start()

    def start_last_of_two():
        @pl.when(depth == 2)
        def _():
            last_copy(0).start()
            relay_in_copy(0).start()

    def pass_on(j):
        @pl.when(depth == 1)
        def _():
            relay_in_copy(j).wait_recv()
            relay_out_copy(j).start()

    def deliver(k):
        @pl.when(k // GROUP == depth)
        def _():
            grads[lax.rem(k, GROUP), depth] = piece_stage[k]

        @pl.when(lax.rem(k, GROUP) == GROUP - 1)
        def _():
            start_piece(k)

        @pl.when(k == 4)
        def _():
            start_piece(10)

    def backward(i, carry):
        k = last - i
        bent = collect(k, load(waves, SLICES))
        store(waves, SLICES, sandwich(bent, step_right[...], step_left[...]))
        deliver(k)
        return carry

    lax.fori_loop(0, last, backward, 0)
    entry = collect(0, load(waves, SLICES))
    deliver(0)

    quarter = PIX // n_depth
    height = 4 * quarter // ring
    for c in range(2):
        for m in range(2):
            value = entry[c][m] if c == 0 else -entry[c][m]
            for d in range(n_depth):
                for i in range(0, quarter, 8):
                    flat = (c * 2 + m) * quarter + i
                    part = flat // height
                    parts[part % 2, part // 2, d, flat % height : flat % height + 8] = value[
                        d * quarter + i : d * quarter + i + 8
                    ]

    core_copy = send(parts.at[1 - core], core_recv, core_sem.at[0], core_sem.at[1], tile + 1 - 2 * core, depth)

    def column_copy(i):
        to = column_peer(i)
        return send(
            column.at[to], column_recv.at[column_spot], column_send_sem.at[to], column_recv_sem.at[column_spot],
            ring_base + 2 * to + core, depth,
        )

    def plane_copy(i):
        to = plane_peer(i)
        to_tile, to_depth = plane_device(to)
        return send(
            plane.at[to_depth], plane_recv.at[plane_spot], plane_send_sem.at[to], plane_recv_sem.at[plane_spot],
            to_tile, to_depth,
        )

    def final_copy(i):
        to = ring_peer(i)
        return send(
            final.at[spot], final.at[spot], final_send_sem.at[to], final_recv_sem.at[spot],
            ring_base + to, depth,
        )

    def start_all(copy, count):
        lax.fori_loop(1, count, lambda i, c: (copy(i).start(), c)[1], 0)

    def wait_sent(copy, count):
        lax.fori_loop(1, count, lambda i, c: (copy(i).wait_send(), c)[1], 0)

    def wait_got(buffer, send_sem, recv_sem, peer, count):
        def one(i, carry):
            frm = peer(i)
            send(buffer.at[frm], buffer.at[frm], send_sem.at[frm], recv_sem.at[frm], tile, depth).wait_recv()
            return carry

        lax.fori_loop(1, count, one, 0)

    def next_copy(j, c):
        return send(
            next_sum.at[j, c], next_recv.at[j, c], next_send_sem.at[j, c], next_recv_sem.at[j, c], after, depth
        )

    def arrived(j, i):
        frm = depth_peer(i)
        sem = grad_recv_sem.at[j, frm]
        send(grads.at[j, frm], grads.at[j, frm], sem, sem, tile, depth).wait_recv()

    def half_arrived(c, i):
        frm = depth_peer(i)
        sem = last_recv_sem.at[frm, c]
        send(grads.at[0, frm, c], grads.at[0, frm, c], sem, sem, tile, depth).wait_recv()

    def gather_half(j, c):
        sums = [0.0] * 4
        for slot in range(n_depth):
            own_row, left_col = row_iota >= row_ref[slot], col_iota >= col_ref[slot]
            block = grads[j, slot, c]
            upper = jnp.where(own_row, block, 0.0)
            lower = block - upper
            upper_left = jnp.where(left_col, upper, 0.0)
            lower_left = jnp.where(left_col, lower, 0.0)
            terms = (upper_left, upper - upper_left, lower_left, lower - lower_left)
            sums = [a + b for a, b in zip(sums, terms)]
        own_sum[j, c, :, :PIX] = sums[0]
        own_sum[j, c, :, PIX:] = sums[1]
        next_sum[j, c, :, :PIX] = sums[2]
        next_sum[j, c, :, PIX:] = sums[3]
        next_copy(j, c).start()

    def gather_slice(j):
        if j == 2:
            for i in range(1, n_depth):
                arrived(j, i)
        elif j == 1:
            arrived(j, 1)
            arrived(j, 3)

            @pl.when(depth == 0)
            def _():
                for c in range(2):
                    sem, half = half_recv_sem.at[c], grads.at[1, 2, c]
                    send(half, half, sem, sem, tile, depth).wait_recv()

            @pl.when(depth != 0)
            def _():
                arrived(j, 2)

        else:
            @pl.when(depth != 0)
            def _():
                for i in range(1, n_depth):
                    arrived(j, i)

        def half(c, carry):
            if j == 0:
                @pl.when(depth == 0)
                def _():
                    for i in range(1, n_depth):
                        half_arrived(c, i)

            gather_half(j, c)
            return carry

        lax.fori_loop(0, 2, half, 0)

    def object_store(j, c):
        return pltpu.make_async_copy(own_sum.at[j, c], (new_real, new_imag)[c].at[j], store_sem.at[j, c])

    def probe_store(c):
        return pltpu.make_async_copy(new_probe.at[c], (new_probe_real, new_probe_imag)[c], store_sem.at[GROUP, c])

    def finish_slice(j):
        for c in range(2):
            next_copy(j, c).wait_recv()
            own_sum[j, c] = objects[c][j] - OBJ_STEP * (own_sum[j, c] + next_recv[j, c])
            object_store(j, c).start()

    core_copy.start()
    start_piece_one()
    core_copy.wait_recv()
    for n in range(n_column):
        column[n] = parts[core, n] + core_recv[n]
    column_recv[column_spot] = column[column_spot]
    start_all(column_copy, n_column)
    for k in (4, 7, 9):
        start_piece(k)
    for j in range(GROUP):
        for c in range(2):
            head_copy(j, c).wait_send()
        for i in range(1, n_depth):
            for c in range(2):
                patch_copy(j, c, depth_peer(i)).wait_send()

    gather_slice(2)

    wait_got(column_recv, column_send_sem, column_recv_sem, column_peer, n_column)
    total = column_recv[0]
    for i in range(1, n_column):
        total = total + column_recv[i]
    plane[...] = total
    plane_recv[plane_spot] = plane[depth]
    start_all(plane_copy, n_line * n_depth)
    start_last(0)
    start_last_of_two()
    pass_on(1)
    for k in (3, 6):
        start_piece(k)
    gather_slice(1)

    wait_got(plane_recv, plane_send_sem, plane_recv_sem, plane_peer, n_line * n_depth)
    total = plane_recv[0]
    for i in range(1, n_line * n_depth):
        total = total + plane_recv[i]
    final[spot] = total
    start_all(final_copy, ring)
    start_last(1)
    pass_on(0)
    gather_slice(0)
    finish_slice(2)
    finish_slice(1)
    for j in (2, 1):
        for c in range(2):
            next_copy(j, c).wait_send()

    def piece_sent(k, carry):
        @pl.when(k // GROUP != depth)
        def _():
            piece_copy(k).wait_send()

        return carry

    lax.fori_loop(2, SLICES, piece_sent, 0)

    @pl.when(lax.rem(depth, 2) == 1)
    def _():
        piece_copy(1).wait_send()
        last_copy(0).wait_send()
        last_copy(1).wait_send()

    @pl.when(depth == 2)
    def _():
        half_copy().wait_send()
        last_copy(0).wait_send()
        relay_in_copy(0).wait_send()
        relay_in_copy(1).wait_send()

    @pl.when(depth == 1)
    def _():
        relay_out_copy(0).wait_send()
        relay_out_copy(1).wait_send()

    core_copy.wait_send()
    wait_sent(column_copy, n_column)
    wait_sent(plane_copy, n_line * n_depth)
    live_total = lax.fori_loop(0, n_tile, lambda i, acc: acc + count_ref[i], 0).astype(jnp.float32)
    wait_got(final, final_send_sem, final_recv_sem, ring_peer, ring)
    for c, source in ((0, probe_real), (1, probe_imag)):
        for m in range(2):
            for i in range(0, quarter, 8):
                flat = (c * 2 + m) * quarter + i
                grad = final[flat // height, flat % height : flat % height + 8]
                start = pl.multiple_of(depth * quarter + i, 8)
                new_probe[c, m, i : i + 8] = source[m, pl.ds(start, 8)] - PROBE_STEP * grad / live_total
        probe_store(c).start()
    finish_slice(0)
    for c in range(2):
        next_copy(0, c).wait_send()
    wait_sent(final_copy, ring)
    for c in range(2):
        for j in range(GROUP):
            object_store(j, c).wait()
        probe_store(c).wait()


def hand_over(*refs):
    sources, targets, held, load_sem, store_sem = refs[:4], refs[4:8], refs[8:12], refs[12], refs[13]
    chunks = []
    for i in range(4):
        for n in range(sources[i].shape[0]):
            at = (i, n)
            chunks.append((
                pltpu.make_async_copy(sources[i].at[n], held[i].at[n], load_sem.at[at]),
                pltpu.make_async_copy(held[i].at[n], targets[i].at[n], store_sem.at[at]),
            ))
    for load, _ in chunks:
        load.start()
    for load, store in chunks:
        load.wait()
        store.start()
    for _, store in chunks:
        store.wait()


def body(
    object_real, object_imag, probe_real, probe_imag, measured, row_offset, col_offset, counts
):
    n_tile, n_depth = lax.axis_size("tile"), lax.axis_size("depth")
    ring = min(RING, n_tile // 2)
    n_line = n_tile // ring
    slab = object_real.shape
    cols = slab[2]
    height = PIX // ring
    hbm = pl.BlockSpec(memory_space=pltpu.HBM)
    smem = pltpu.SMEM
    f32 = jnp.float32
    dma = pltpu.SemaphoreType.DMA
    results = pl.pallas_call(
        functools.partial(kernel, n_tile, n_depth, ring),
        out_shape=(
            jax.ShapeDtypeStruct(slab, f32),
            jax.ShapeDtypeStruct(slab, f32),
            jax.ShapeDtypeStruct((2, PIX // n_depth, PIX), f32),
            jax.ShapeDtypeStruct((2, PIX // n_depth, PIX), f32),
        ),
        in_specs=[hbm] * 9,
        out_specs=(hbm,) * 4,
        scratch_shapes=[
            pltpu.VMEM((GROUP, 2, PIX, cols), f32),
            pltpu.VMEM((GROUP, n_depth, 2, PIX, PIX), f32),
            pltpu.VMEM((SLICES, 2, PIX, PIX), f32),
            pltpu.VMEM((SLICES + 1, 2, 2, PIX, PIX), f32),
            pltpu.VMEM((SLICES, 2, PIX, PIX), f32),
            pltpu.VMEM((GROUP, n_depth, 2, PIX, PIX), f32),
            pltpu.VMEM((GROUP, 2, PIX, cols), f32),
            pltpu.VMEM((GROUP, 2, PIX, cols), f32),
            pltpu.VMEM((GROUP, 2, PIX, cols), f32),
            pltpu.VMEM((2, ring // 2, n_depth, height, PIX), f32),
            pltpu.VMEM((ring // 2, n_depth, height, PIX), f32),
            pltpu.VMEM((ring // 2, n_depth, height, PIX), f32),
            pltpu.VMEM((ring // 2, n_depth, height, PIX), f32),
            pltpu.VMEM((n_depth, height, PIX), f32),
            pltpu.VMEM((n_line * n_depth, height, PIX), f32),
            pltpu.VMEM((ring, height, PIX), f32),
            smem(row_offset.shape, jnp.int32), smem(col_offset.shape, jnp.int32), smem(counts.shape, jnp.int32),
            pltpu.VMEM(slab, f32), pltpu.VMEM(slab, f32),
            pltpu.VMEM(probe_real.shape, f32), pltpu.VMEM(probe_real.shape, f32),
            pltpu.VMEM(measured.shape[1:], f32),
            *[pltpu.VMEM(s, jnp.bfloat16) for s in ((6 * PIX, 2 * PIX), (2 * PIX, 6 * PIX))] * 2,
            pltpu.VMEM((4, PIX, PIX), f32), dma((9,)),
            pltpu.VMEM((2, 2, PIX // n_depth, PIX), f32), dma((GROUP + 1, 2)),
            dma((GROUP, 2)), dma((GROUP, 2)), dma((GROUP, n_depth, 2)), dma((SLICES, 2)),
            dma((SLICES,)), dma((GROUP, n_depth)), dma((GROUP, 2)), dma((GROUP, 2)),
            dma((2,)), dma((ring // 2,)), dma((ring // 2,)),
            dma((n_line * n_depth,)), dma((n_line * n_depth,)), dma((ring,)), dma((ring,)),
            dma((2,)), dma((n_depth, 2)), pltpu.VMEM((2, PIX, PIX), f32),
            dma((1,)), dma((2,)), dma((2,)), dma((2,)), dma((2,)),
        ],
        compiler_params=pltpu.CompilerParams(
            collective_id=0, has_side_effects=True, vmem_limit_bytes=60 * 1024 * 1024
        ),
    )(
        row_offset, col_offset, counts, object_real, object_imag, probe_real, probe_imag, measured,
        jnp.asarray(make_constants()),
    )
    return pl.pallas_call(
        hand_over,
        out_shape=tuple(jax.ShapeDtypeStruct(r.shape, r.dtype) for r in results),
        in_specs=[hbm] * 4,
        out_specs=(hbm,) * 4,
        scratch_shapes=[pltpu.VMEM(r.shape, r.dtype) for r in results] + [dma((4, GROUP)), dma((4, GROUP))],
        compiler_params=pltpu.CompilerParams(vmem_limit_bytes=60 * 1024 * 1024),
    )(*results)


def solution(mesh):
    placed = (
        P("depth", "tile", None),
        P("depth", "tile", None),
        P(),
        P(),
        P("tile", None, None),
        P("tile"),
        P("tile"),
        P(),
    )
    return jax.shard_map(
        body,
        mesh=mesh,
        in_specs=placed,
        out_specs=(
            P("depth", "tile", None),
            P("depth", "tile", None),
            P(None, "depth", None),
            P(None, "depth", None),
        ),
        check_vma=False,
    )
```

```python
import functools

import jax
import jax.numpy as jnp
import numpy as np
from jax import lax
from jax.experimental import pallas as pl
from jax.experimental.pallas import tpu as pltpu
from jax.sharding import PartitionSpec as P

PIX = 128
SLICES = 12
GROUP = 3
RING = 16
PROP_PHASE = 12.0
AMP_EPS = 0.05
OBJ_STEP = 1.0
PROBE_STEP = 4.0


def make_constants():
    n = np.arange(PIX)
    dft = np.exp(-2j * np.pi * ((n[:, None] * n[None, :]) % PIX) / PIX) / np.sqrt(PIX)
    freq = ((n + PIX // 2) % PIX - PIX // 2) / PIX
    step = np.conj(dft) @ (np.exp(-1j * PROP_PHASE * freq**2)[:, None] * dft)
    return np.stack([step.real, step.imag, dft.real, dft.imag]).astype(np.float32)


def split(value):
    high = value.astype(jnp.bfloat16)
    low = (value - high.astype(jnp.float32)).astype(jnp.bfloat16)
    return high, low


def make_factors(real, imag, right, left):
    for i, line in enumerate(((real, imag), (-imag, real))):
        high, low = split(jnp.concatenate(line, axis=1))
        for n, part in enumerate((high, high, low)):
            right[2 * n * PIX + i * PIX : 2 * n * PIX + (i + 1) * PIX] = part
    for i, line in enumerate(((real, -imag), (imag, real))):
        high, low = split(jnp.concatenate(line, axis=1))
        for n, part in enumerate((high, high, low)):
            left[i * PIX : (i + 1) * PIX, 2 * n * PIX : 2 * (n + 1) * PIX] = part


def sandwich(field, right, left):
    middle = []
    for m in range(2):
        high, low = split(jnp.concatenate([field[0][m], field[1][m]], axis=1))
        wide = jnp.concatenate([high, low, high], axis=1)
        middle.append(jnp.dot(wide, right, preferred_element_type=jnp.float32))
    done = []
    for m in range(2):
        high, low = split(jnp.concatenate([middle[m][:, :PIX], middle[m][:, PIX:]], axis=0))
        tall = jnp.concatenate([high, low, high], axis=0)
        done.append(jnp.dot(left, tall, preferred_element_type=jnp.float32))
    return [[done[m][c * PIX : (c + 1) * PIX] for m in range(2)] for c in range(2)]


def times(patch_real, patch_imag, field):
    real = [field[0][m] * patch_real - field[1][m] * patch_imag for m in range(2)]
    imag = [field[0][m] * patch_imag + field[1][m] * patch_real for m in range(2)]
    return [real, imag]


MESH = pl.DeviceIdType.MESH


def turned(block, rows, cols):
    return pltpu.roll(pltpu.roll(block, rows, 0), cols, 1)


def kernel(
    n_tile, n_depth, ring,
    row_hbm, col_hbm, count_hbm, real_hbm, imag_hbm, probe_real_hbm, probe_imag_hbm, measured_hbm,
    table_hbm,
    new_real, new_imag, new_probe_real, new_probe_imag,
    head, stage, patch_ref, waves, piece_stage, grads, own_sum, next_sum, next_recv,
    parts, core_recv, column, column_recv, plane, plane_recv, final,
    row_ref, col_ref, count_ref, obj_real, obj_imag, probe_real, probe_imag, measured_ref,
    step_right, step_left, dft_right, dft_left, table, load_sem, new_probe, store_sem,
    head_send_sem, head_recv_sem, patch_send_sem, patch_recv_sem, piece_send_sem, grad_recv_sem,
    next_send_sem, next_recv_sem,
    core_sem, column_send_sem, column_recv_sem, plane_send_sem, plane_recv_sem, final_send_sem, final_recv_sem,
    last_send_sem, last_recv_sem, relay, half_send_sem, half_recv_sem, in_send_sem, in_recv_sem, out_send_sem,
):
    objects = (obj_real, obj_imag)
    sources = (real_hbm, imag_hbm)
    tile = lax.axis_index("tile")
    depth = lax.axis_index("depth")

    after, before = lax.rem(tile + 1, n_tile), lax.rem(tile + n_tile - 1, n_tile)
    n_line = n_tile // ring
    spot, row_of = lax.rem(tile, ring), tile // ring
    ring_base = row_of * ring

    def send(src, dst, send_sem, recv_sem, to_tile, to_depth):
        return pltpu.make_async_remote_copy(
            src_ref=src, dst_ref=dst, send_sem=send_sem, recv_sem=recv_sem,
            device_id=(to_tile, to_depth), device_id_type=MESH,
        )

    def ring_peer(i):
        return lax.rem(spot + i, ring)

    plane_spot = row_of * n_depth + depth

    def plane_peer(i):
        return lax.rem(plane_spot + i, n_line * n_depth)

    def plane_device(n):
        return (n // n_depth) * ring + spot, lax.rem(n, n_depth)

    core, column_spot, n_column = lax.rem(spot, 2), spot // 2, ring // 2

    def column_peer(i):
        return lax.rem(column_spot + i, n_column)

    def depth_peer(i):
        return lax.rem(depth + i, n_depth)

    barrier = pltpu.get_barrier_semaphore()

    def greet(to_tile, to_depth):
        pl.semaphore_signal(barrier, inc=1, device_id=(to_tile, to_depth), device_id_type=MESH)

    greet(after, depth)
    greet(before, depth)
    lax.fori_loop(1, ring, lambda i, c: (greet(ring_base + ring_peer(i), depth), c)[1], 0)
    lax.fori_loop(1, n_line * n_depth, lambda i, c: (greet(*plane_device(plane_peer(i))), c)[1], 0)
    def fetch(n, src, dst):
        copy = pltpu.make_async_copy(src, dst, load_sem.at[n])
        copy.start()
        return copy

    offset_loads = [fetch(0, row_hbm, row_ref), fetch(1, col_hbm, col_ref)]
    object_loads = [fetch(2, real_hbm, obj_real), fetch(3, imag_hbm, obj_imag)]
    probe_loads = [fetch(4, probe_real_hbm, probe_real), fetch(5, probe_imag_hbm, probe_imag)]
    table_loads = [fetch(6, table_hbm, table)]
    far_loads = [fetch(7, measured_hbm.at[depth], measured_ref), fetch(8, count_hbm, count_ref)]

    def loaded(copies):
        for copy in copies:
            copy.wait()

    pl.semaphore_wait(barrier, 2 + ring - 1 + n_line * n_depth - 1)

    def head_copy(j, c):
        return send(sources[c].at[j], head.at[j, c], head_send_sem.at[j, c], head_recv_sem.at[j, c], before, depth)

    def start_head(j):
        for c in range(2):
            head_copy(j, c).start()

    start_head(0)

    row_iota = lax.broadcasted_iota(jnp.int32, (PIX, PIX), 0)
    col_iota = lax.broadcasted_iota(jnp.int32, (PIX, PIX), 1)

    def patch_copy(j, c, to):
        k = depth * GROUP + j
        return send(
            stage.at[j, to, c], patch_ref.at[k, c], patch_send_sem.at[j, to, c], patch_recv_sem.at[k, c], tile, to
        )

    def cut(j, c, i):
        slot = depth_peer(i)
        row, col = row_ref[slot], col_ref[slot]
        own_row, left_col = row_iota >= row, col_iota >= col
        upper = jnp.where(left_col, objects[c][j, :, :PIX], objects[c][j, :, PIX:])
        lower = jnp.where(left_col, head[j, c, :, :PIX], head[j, c, :, PIX:])
        block = jnp.where(own_row, upper, lower)
        return turned(block, lax.rem(PIX - row, PIX), lax.rem(PIX - col + PIX, PIX))

    def cut_slice(j, carry):
        for c in range(2):
            head_copy(j, c).wait_recv()
            if c == 1:
                @pl.when(j + 1 < GROUP)
                def _():
                    start_head(j + 1)

            for i in (2, 1, 3):
                slot = depth_peer(i)
                stage[j, slot, c] = cut(j, c, i)
                patch_copy(j, c, slot).start()
            patch_ref[depth * GROUP + j, c] = cut(j, c, 0)
        return carry

    loaded(offset_loads)
    loaded(object_loads)
    lax.fori_loop(0, GROUP, cut_slice, 0)

    def load(ref, k):
        return [[ref[k, c, m] for m in range(2)] for c in range(2)]

    def store(ref, k, field):
        for c in range(2):
            for m in range(2):
                ref[k, c, m] = field[c][m]

    def patch_ready(k):
        @pl.when(k // GROUP != depth)
        def _():
            for c in range(2):
                sem = patch_recv_sem.at[k, c]
                send(stage.at[0, 0, 0], patch_ref.at[k, c], sem, sem, tile, depth).wait_recv()

    loaded(probe_loads)
    loaded(table_loads)
    make_factors(table[0], table[1], step_right, step_left)
    make_factors(table[2], table[3], dft_right, dft_left)
    store(waves, 0, [[probe_real[m] for m in range(2)], [probe_imag[m] for m in range(2)]])

    def forward(k, carry):
        patch_ready(k)

        chi = times(patch_ref[k, 0], patch_ref[k, 1], load(waves, k))
        store(waves, k + 1, sandwich(chi, step_right[...], step_left[...]))
        return carry

    last = SLICES - 1
    lax.fori_loop(0, last, forward, 0)
    patch_ready(last)
    loaded(far_loads)
    exit_wave = times(patch_ref[last, 0], patch_ref[last, 1], load(waves, last))
    far = sandwich(exit_wave, dft_right[...], dft_left[...])
    intensity = sum(far[c][m] * far[c][m] for c in range(2) for m in range(2))
    live = jnp.where(depth < count_ref[tile], 1.0, 0.0)
    factor = (1.0 - measured_ref[...] * lax.rsqrt(intensity + AMP_EPS)) * live
    bent = [[far[0][m] * factor for m in range(2)], [-far[1][m] * factor for m in range(2)]]
    store(waves, SLICES, sandwich(bent, dft_right[...], dft_left[...]))

    own_turn = (row_ref[depth], col_ref[depth])

    def collect(k, grad):
        wave = load(waves, k)
        real = sum(wave[0][m] * grad[0][m] - wave[1][m] * grad[1][m] for m in range(2))
        imag = -sum(wave[0][m] * grad[1][m] + wave[1][m] * grad[0][m] for m in range(2))
        row, col = own_turn
        piece_stage[k, 0] = turned(real, row, lax.rem(col, PIX))
        piece_stage[k, 1] = turned(imag, row, lax.rem(col, PIX))
        return times(patch_ref[k, 0], patch_ref[k, 1], grad)

    def piece_copy(k):
        j = lax.rem(k, GROUP)
        return send(
            piece_stage.at[k], grads.at[j, depth], piece_send_sem.at[k], grad_recv_sem.at[j, depth], tile, k // GROUP
        )

    def last_copy(c):
        return send(
            piece_stage.at[0, c], grads.at[0, depth, c], last_send_sem.at[c], last_recv_sem.at[depth, c], tile, 0
        )

    def half_copy():
        return send(
            piece_stage.at[1, 0], grads.at[1, depth, 0], half_send_sem.at[0], half_recv_sem.at[0], tile, 0
        )

    def relay_in_copy(j):
        return send(piece_stage.at[j, 1], relay.at[j], in_send_sem.at[j], in_recv_sem.at[j], tile, 1)

    def relay_out_copy(j):
        sem = last_recv_sem.at[2, 1] if j == 0 else half_recv_sem.at[1]
        return send(relay.at[j], grads.at[j, 2, 1], out_send_sem.at[j], sem, tile, 0)

    def start_piece(k):
        @pl.when(k // GROUP != depth)
        def _():
            piece_copy(k).start()

    def start_piece_one():
        @pl.when(lax.rem(depth, 2) == 1)
        def _():
            piece_copy(1).start()

        @pl.when(depth == 2)
        def _():
            half_copy().start()
            relay_in_copy(1).start()

    def start_last(c):
        @pl.when(lax.rem(depth, 2) == 1)
        def _():
            last_copy(c).start()

    def start_last_of_two():
        @pl.when(depth == 2)
        def _():
            last_copy(0).start()
            relay_in_copy(0).start()

    def pass_on(j):
        @pl.when(depth == 1)
        def _():
            relay_in_copy(j).wait_recv()
            relay_out_copy(j).start()

    def deliver(k):
        @pl.when(k // GROUP == depth)
        def _():
            grads[lax.rem(k, GROUP), depth] = piece_stage[k]

        @pl.when(lax.rem(k, GROUP) == GROUP - 1)
        def _():
            start_piece(k)

        @pl.when(k == 4)
        def _():
            start_piece(10)

    def backward(i, carry):
        k = last - i
        bent = collect(k, load(waves, SLICES))
        store(waves, SLICES, sandwich(bent, step_right[...], step_left[...]))
        deliver(k)
        return carry

    lax.fori_loop(0, last, backward, 0)
    entry = collect(0, load(waves, SLICES))
    deliver(0)

    quarter = PIX // n_depth
    height = 4 * quarter // ring
    for c in range(2):
        for m in range(2):
            value = entry[c][m] if c == 0 else -entry[c][m]
            for d in range(n_depth):
                for i in range(0, quarter, 8):
                    flat = (c * 2 + m) * quarter + i
                    part = flat // height
                    parts[part % 2, part // 2, d, flat % height : flat % height + 8] = value[
                        d * quarter + i : d * quarter + i + 8
                    ]

    core_copy = send(parts.at[1 - core], core_recv, core_sem.at[0], core_sem.at[1], tile + 1 - 2 * core, depth)

    def column_copy(i):
        to = column_peer(i)
        return send(
            column.at[to], column_recv.at[column_spot], column_send_sem.at[to], column_recv_sem.at[column_spot],
            ring_base + 2 * to + core, depth,
        )

    def plane_copy(i):
        to = plane_peer(i)
        to_tile, to_depth = plane_device(to)
        return send(
            plane.at[to_depth], plane_recv.at[plane_spot], plane_send_sem.at[to], plane_recv_sem.at[plane_spot],
            to_tile, to_depth,
        )

    def final_copy(i):
        to = ring_peer(i)
        return send(
            final.at[spot], final.at[spot], final_send_sem.at[to], final_recv_sem.at[spot],
            ring_base + to, depth,
        )

    def start_all(copy, count):
        lax.fori_loop(1, count, lambda i, c: (copy(i).start(), c)[1], 0)

    def wait_sent(copy, count):
        lax.fori_loop(1, count, lambda i, c: (copy(i).wait_send(), c)[1], 0)

    def wait_got(buffer, send_sem, recv_sem, peer, count):
        def one(i, carry):
            frm = peer(i)
            send(buffer.at[frm], buffer.at[frm], send_sem.at[frm], recv_sem.at[frm], tile, depth).wait_recv()
            return carry

        lax.fori_loop(1, count, one, 0)

    def next_copy(j, c):
        return send(
            next_sum.at[j, c], next_recv.at[j, c], next_send_sem.at[j, c], next_recv_sem.at[j, c], after, depth
        )

    def arrived(j, i):
        frm = depth_peer(i)
        sem = grad_recv_sem.at[j, frm]
        send(grads.at[j, frm], grads.at[j, frm], sem, sem, tile, depth).wait_recv()

    def half_arrived(c, i):
        frm = depth_peer(i)
        sem = last_recv_sem.at[frm, c]
        send(grads.at[0, frm, c], grads.at[0, frm, c], sem, sem, tile, depth).wait_recv()

    def gather_half(j, c):
        sums = [0.0] * 4
        for slot in range(n_depth):
            own_row, left_col = row_iota >= row_ref[slot], col_iota >= col_ref[slot]
            block = grads[j, slot, c]
            upper = jnp.where(own_row, block, 0.0)
            lower = block - upper
            upper_left = jnp.where(left_col, upper, 0.0)
            lower_left = jnp.where(left_col, lower, 0.0)
            terms = (upper_left, upper - upper_left, lower_left, lower - lower_left)
            sums = [a + b for a, b in zip(sums, terms)]
        own_sum[j, c, :, :PIX] = sums[0]
        own_sum[j, c, :, PIX:] = sums[1]
        next_sum[j, c, :, :PIX] = sums[2]
        next_sum[j, c, :, PIX:] = sums[3]
        next_copy(j, c).start()

    def gather_slice(j):
        if j == 2:
            for i in range(1, n_depth):
                arrived(j, i)
        elif j == 1:
            arrived(j, 1)
            arrived(j, 3)

            @pl.when(depth == 0)
            def _():
                for c in range(2):
                    sem, half = half_recv_sem.at[c], grads.at[1, 2, c]
                    send(half, half, sem, sem, tile, depth).wait_recv()

            @pl.when(depth != 0)
            def _():
                arrived(j, 2)

        else:
            @pl.when(depth != 0)
            def _():
                for i in range(1, n_depth):
                    arrived(j, i)

        def half(c, carry):
            if j == 0:
                @pl.when(depth == 0)
                def _():
                    for i in range(1, n_depth):
                        half_arrived(c, i)

            gather_half(j, c)
            return carry

        lax.fori_loop(0, 2, half, 0)

    def object_store(j, c):
        return pltpu.make_async_copy(own_sum.at[j, c], (new_real, new_imag)[c].at[j], store_sem.at[j, c])

    def probe_store(c):
        return pltpu.make_async_copy(new_probe.at[c], (new_probe_real, new_probe_imag)[c], store_sem.at[GROUP, c])

    def finish_slice(j):
        for c in range(2):
            next_copy(j, c).wait_recv()
            own_sum[j, c] = objects[c][j] - OBJ_STEP * (own_sum[j, c] + next_recv[j, c])
            object_store(j, c).start()

    core_copy.start()
    start_piece_one()
    core_copy.wait_recv()
    for n in range(n_column):
        column[n] = parts[core, n] + core_recv[n]
    column_recv[column_spot] = column[column_spot]
    start_all(column_copy, n_column)
    for k in (4, 7, 9):
        start_piece(k)
    for j in range(GROUP):
        for c in range(2):
            head_copy(j, c).wait_send()
        for i in range(1, n_depth):
            for c in range(2):
                patch_copy(j, c, depth_peer(i)).wait_send()

    gather_slice(2)

    wait_got(column_recv, column_send_sem, column_recv_sem, column_peer, n_column)
    total = column_recv[0]
    for i in range(1, n_column):
        total = total + column_recv[i]
    plane[...] = total
    plane_recv[plane_spot] = plane[depth]
    start_all(plane_copy, n_line * n_depth)
    start_last(0)
    start_last_of_two()
    pass_on(1)
    for k in (3, 6):
        start_piece(k)
    gather_slice(1)
    start_last(1)

    wait_got(plane_recv, plane_send_sem, plane_recv_sem, plane_peer, n_line * n_depth)
    total = plane_recv[0]
    for i in range(1, n_line * n_depth):
        total = total + plane_recv[i]
    final[spot] = total
    start_all(final_copy, ring)
    pass_on(0)
    gather_slice(0)
    finish_slice(2)
    finish_slice(1)
    for j in (2, 1):
        for c in range(2):
            next_copy(j, c).wait_send()

    def piece_sent(k, carry):
        @pl.when(k // GROUP != depth)
        def _():
            piece_copy(k).wait_send()

        return carry

    lax.fori_loop(2, SLICES, piece_sent, 0)

    @pl.when(lax.rem(depth, 2) == 1)
    def _():
        piece_copy(1).wait_send()
        last_copy(0).wait_send()
        last_copy(1).wait_send()

    @pl.when(depth == 2)
    def _():
        half_copy().wait_send()
        last_copy(0).wait_send()
        relay_in_copy(0).wait_send()
        relay_in_copy(1).wait_send()

    @pl.when(depth == 1)
    def _():
        relay_out_copy(0).wait_send()
        relay_out_copy(1).wait_send()

    core_copy.wait_send()
    wait_sent(column_copy, n_column)
    wait_sent(plane_copy, n_line * n_depth)
    live_total = lax.fori_loop(0, n_tile, lambda i, acc: acc + count_ref[i], 0).astype(jnp.float32)
    wait_got(final, final_send_sem, final_recv_sem, ring_peer, ring)
    for c, source in ((0, probe_real), (1, probe_imag)):
        for m in range(2):
            for i in range(0, quarter, 8):
                flat = (c * 2 + m) * quarter + i
                grad = final[flat // height, flat % height : flat % height + 8]
                start = pl.multiple_of(depth * quarter + i, 8)
                new_probe[c, m, i : i + 8] = source[m, pl.ds(start, 8)] - PROBE_STEP * grad / live_total
        probe_store(c).start()
    finish_slice(0)
    for c in range(2):
        next_copy(0, c).wait_send()
    wait_sent(final_copy, ring)
    for c in range(2):
        for j in range(GROUP):
            object_store(j, c).wait()
        probe_store(c).wait()


def hand_over(*refs):
    sources, targets, held, load_sem, store_sem = refs[:4], refs[4:8], refs[8:12], refs[12], refs[13]
    chunks = []
    for i in range(4):
        for n in range(sources[i].shape[0]):
            at = (i, n)
            chunks.append((
                pltpu.make_async_copy(sources[i].at[n], held[i].at[n], load_sem.at[at]),
                pltpu.make_async_copy(held[i].at[n], targets[i].at[n], store_sem.at[at]),
            ))
    for load, _ in chunks:
        load.start()
    for load, store in chunks:
        load.wait()
        store.start()
    for _, store in chunks:
        store.wait()


def body(
    object_real, object_imag, probe_real, probe_imag, measured, row_offset, col_offset, counts
):
    n_tile, n_depth = lax.axis_size("tile"), lax.axis_size("depth")
    ring = min(RING, n_tile // 2)
    n_line = n_tile // ring
    slab = object_real.shape
    cols = slab[2]
    height = PIX // ring
    hbm = pl.BlockSpec(memory_space=pltpu.HBM)
    smem = pltpu.SMEM
    f32 = jnp.float32
    dma = pltpu.SemaphoreType.DMA
    results = pl.pallas_call(
        functools.partial(kernel, n_tile, n_depth, ring),
        out_shape=(
            jax.ShapeDtypeStruct(slab, f32),
            jax.ShapeDtypeStruct(slab, f32),
            jax.ShapeDtypeStruct((2, PIX // n_depth, PIX), f32),
            jax.ShapeDtypeStruct((2, PIX // n_depth, PIX), f32),
        ),
        in_specs=[hbm] * 9,
        out_specs=(hbm,) * 4,
        scratch_shapes=[
            pltpu.VMEM((GROUP, 2, PIX, cols), f32),
            pltpu.VMEM((GROUP, n_depth, 2, PIX, PIX), f32),
            pltpu.VMEM((SLICES, 2, PIX, PIX), f32),
            pltpu.VMEM((SLICES + 1, 2, 2, PIX, PIX), f32),
            pltpu.VMEM((SLICES, 2, PIX, PIX), f32),
            pltpu.VMEM((GROUP, n_depth, 2, PIX, PIX), f32),
            pltpu.VMEM((GROUP, 2, PIX, cols), f32),
            pltpu.VMEM((GROUP, 2, PIX, cols), f32),
            pltpu.VMEM((GROUP, 2, PIX, cols), f32),
            pltpu.VMEM((2, ring // 2, n_depth, height, PIX), f32),
            pltpu.VMEM((ring // 2, n_depth, height, PIX), f32),
            pltpu.VMEM((ring // 2, n_depth, height, PIX), f32),
            pltpu.VMEM((ring // 2, n_depth, height, PIX), f32),
            pltpu.VMEM((n_depth, height, PIX), f32),
            pltpu.VMEM((n_line * n_depth, height, PIX), f32),
            pltpu.VMEM((ring, height, PIX), f32),
            smem(row_offset.shape, jnp.int32), smem(col_offset.shape, jnp.int32), smem(counts.shape, jnp.int32),
            pltpu.VMEM(slab, f32), pltpu.VMEM(slab, f32),
            pltpu.VMEM(probe_real.shape, f32), pltpu.VMEM(probe_real.shape, f32),
            pltpu.VMEM(measured.shape[1:], f32),
            *[pltpu.VMEM(s, jnp.bfloat16) for s in ((6 * PIX, 2 * PIX), (2 * PIX, 6 * PIX))] * 2,
            pltpu.VMEM((4, PIX, PIX), f32), dma((9,)),
            pltpu.VMEM((2, 2, PIX // n_depth, PIX), f32), dma((GROUP + 1, 2)),
            dma((GROUP, 2)), dma((GROUP, 2)), dma((GROUP, n_depth, 2)), dma((SLICES, 2)),
            dma((SLICES,)), dma((GROUP, n_depth)), dma((GROUP, 2)), dma((GROUP, 2)),
            dma((2,)), dma((ring // 2,)), dma((ring // 2,)),
            dma((n_line * n_depth,)), dma((n_line * n_depth,)), dma((ring,)), dma((ring,)),
            dma((2,)), dma((n_depth, 2)), pltpu.VMEM((2, PIX, PIX), f32),
            dma((1,)), dma((2,)), dma((2,)), dma((2,)), dma((2,)),
        ],
        compiler_params=pltpu.CompilerParams(
            collective_id=0, has_side_effects=True, vmem_limit_bytes=60 * 1024 * 1024
        ),
    )(
        row_offset, col_offset, counts, object_real, object_imag, probe_real, probe_imag, measured,
        jnp.asarray(make_constants()),
    )
    return pl.pallas_call(
        hand_over,
        out_shape=tuple(jax.ShapeDtypeStruct(r.shape, r.dtype) for r in results),
        in_specs=[hbm] * 4,
        out_specs=(hbm,) * 4,
        scratch_shapes=[pltpu.VMEM(r.shape, r.dtype) for r in results] + [dma((4, GROUP)), dma((4, GROUP))],
        compiler_params=pltpu.CompilerParams(vmem_limit_bytes=60 * 1024 * 1024),
    )(*results)


def solution(mesh):
    placed = (
        P("depth", "tile", None),
        P("depth", "tile", None),
        P(),
        P(),
        P("tile", None, None),
        P("tile"),
        P("tile"),
        P(),
    )
    return jax.shard_map(
        body,
        mesh=mesh,
        in_specs=placed,
        out_specs=(
            P("depth", "tile", None),
            P("depth", "tile", None),
            P(None, "depth", None),
            P(None, "depth", None),
        ),
        check_vma=False,
    )
```
